256 devices in a mesh: dp: 8 (over z), ctx: 32 (over y, x, core).
Axes of the slice: x: 4, y: 4, z: 8, core: 2. Of those that a mesh axis runs over, the one named last changes fastest.
Arguments:
- tokens: bfloat16 [8, 20480, 1024], P('dp', 'ctx'), may hold values from -16 to 16
- slot_keys: bfloat16 [1024, 256], replicated, may hold values from -1 to 1
- w_in: bfloat16 [64, 1024, 4096], P('ctx', None, 'dp'), may hold values from -0.1875 to 0.1875
- w_out: bfloat16 [64, 4096, 1024], P('ctx', 'dp'), may hold values from -0.09375 to 0.09375
- out_grad: bfloat16 [8, 20480, 1024], P('dp', 'ctx'), may hold values from -0.59765625 to 0.59765625
Outputs:
- tokens_grad: bfloat16 [8, 20480, 1024], P('dp', 'ctx')
- slot_keys_grad: float32 [1024, 256], P('ctx')
- w_in_grad: bfloat16 [64, 1024, 4096], P('ctx', None, 'dp')
- w_out_grad: bfloat16 [64, 4096, 1024], P('ctx', 'dp')
The draws below stay inside these ranges and needn't reach their ends.
All inputs are finite; a program needn't handle non-finite values.
Results may differ from the reference program's by a relative error of at most 0.04.
Values may be sent and summed in bfloat16 or wider, within the bound.
A program may use at most 64 MiB of HBM per device.

```python
import jax
import jax.numpy as jnp
from jax import lax

D = 1024
H = 4096
E = 64
CLIPS = 8
CLIP_TOK = 20480
SLOTS = 256


def key_columns(key):
    sigma = 3.0 * D ** (-0.5)
    base_draw = jnp.clip(jax.random.normal(key, (D, SLOTS), jnp.float32), -2.5, 2.5) * sigma
    for strength_index in range(3):
        column = 2 * (strength_index * SLOTS // 6)
        paired = base_draw[:, column + 1]
        base_draw = base_draw.at[:, column + 1].set(paired)
    return base_draw


def draw_slot_keys(key, part):
    columns = key_columns(key)
    return columns.astype(jnp.bfloat16)


def draw_tokens(key, part):
    key = jax.random.fold_in(key, 11)
    position_ramp = 0.6 + 1.2 * jnp.arange(CLIP_TOK, dtype=jnp.float32) / max(CLIP_TOK - 1, 1)
    base_draw = jnp.clip(jax.random.normal(key, (CLIPS, CLIP_TOK, D), jnp.float32), -6.0, 6.0)
    return (base_draw * position_ramp[None, :, None]).astype(jnp.bfloat16)


def level_of(stream_key, extent, pieces, low, largest):
    loudness = 1.0
    for axis_at, shards_of in pieces:
        draws = jax.random.uniform(jax.random.fold_in(jax.random.fold_in(stream_key, 6), axis_at), (shards_of,), jnp.float32, low / len(pieces), largest / len(pieces))
        loudness = loudness * jnp.repeat(jnp.exp(draws), extent[axis_at] // shards_of).reshape((-1,) + (1,) * (len(extent) - 1 - axis_at))
    return loudness


def scatter_about(rng, shape, scale, bound, cuts=(), kind=jnp.bfloat16):
    loudness = level_of(rng, shape, cuts, -0.22, 0.18) if cuts else 1.0
    array = jax.random.normal(rng, shape, jnp.float32) * scale * loudness
    return jnp.minimum(jnp.maximum(array, -bound), bound).astype(kind)


def setup_inputs(seed: int = 0) -> dict:
    key_of = jax.random.split(jax.random.key(seed), 6)
    return {
        "tokens": draw_tokens(jax.random.fold_in(key_of[5], 71), 0),
        "slot_keys": draw_slot_keys(jax.random.fold_in(key_of[5], 71), 0),
        "w_in": scatter_about(key_of[2], (E, D, H), D ** -0.5, 0.1875, ((0, 32), (2, 8))),
        "w_out": scatter_about(key_of[3], (E, H, D), H ** -0.5, 0.09375, ((0, 32), (1, 8))),
        "out_grad": scatter_about(key_of[4], (CLIPS, CLIP_TOK, D), 0.1, 0.59765625, ((0, 8), (1, 32))),
    }


GELU_A = 0.7978845608028654
GELU_B = 0.044715


def gelu_value(value):
    return 0.5 * value * (1.0 + jnp.tanh(GELU_A * (value + GELU_B * value * value * value)))


def gelu_slope(value):
    inner = jnp.tanh(GELU_A * (value + GELU_B * value * value * value))
    return 0.5 * (1.0 + inner) + 0.5 * value * (1.0 - inner * inner) * GELU_A * (1.0 + 3.0 * GELU_B * value * value)


def expert_pass(operands):
    slot_rows, grad_rows, weight_in, weight_out = operands
    pre_act = jnp.dot(slot_rows, weight_in, preferred_element_type=jnp.float32)
    activated = gelu_value(pre_act).astype(jnp.bfloat16)
    produced = jnp.dot(activated, weight_out, preferred_element_type=jnp.float32).astype(jnp.bfloat16)
    act_grad = jnp.dot(grad_rows, weight_out.T, preferred_element_type=jnp.float32)
    pre_grad = (act_grad * gelu_slope(pre_act)).astype(jnp.bfloat16)
    out_weight_grad = jnp.dot(activated.T, grad_rows, preferred_element_type=jnp.float32).astype(jnp.bfloat16)
    in_weight_grad = jnp.dot(slot_rows.T, pre_grad, preferred_element_type=jnp.float32).astype(jnp.bfloat16)
    back = jnp.dot(pre_grad, weight_in.T, preferred_element_type=jnp.float32).astype(jnp.bfloat16)
    return produced, in_weight_grad, out_weight_grad, back


def reference(tokens, slot_keys, w_in, w_out, out_grad):
    clip_count = tokens.shape[0]
    expert_count = w_in.shape[0]
    per_expert = slot_keys.shape[1] // expert_count
    feature_width = tokens.shape[2]
    disp_list = []
    comb_list = []
    slot_in_list = []
    slot_grad_list = []
    for clip_index in range(clip_count):
        logits = jnp.dot(tokens[clip_index], slot_keys, preferred_element_type=jnp.float32)
        disp_prob = jax.nn.softmax(logits, axis=0)
        comb_prob = jax.nn.softmax(logits, axis=1)
        disp_list.append(disp_prob)
        comb_list.append(comb_prob)
        slot_in_list.append(jnp.dot(disp_prob.astype(jnp.bfloat16).T, tokens[clip_index], preferred_element_type=jnp.float32).astype(jnp.bfloat16))
        slot_grad_list.append(jnp.dot(comb_prob.astype(jnp.bfloat16).T, out_grad[clip_index], preferred_element_type=jnp.float32).astype(jnp.bfloat16))

    def to_experts(stacked):
        return stacked.reshape(clip_count, expert_count, per_expert, feature_width).transpose(1, 0, 2, 3).reshape(expert_count, clip_count * per_expert, feature_width)

    def from_experts(grouped):
        return grouped.reshape(expert_count, clip_count, per_expert, feature_width).transpose(1, 0, 2, 3).reshape(clip_count, expert_count * per_expert, feature_width)

    slot_rows = to_experts(jnp.stack(slot_in_list))
    grad_rows = to_experts(jnp.stack(slot_grad_list))
    produced, w_in_grad, w_out_grad, back = lax.map(expert_pass, (slot_rows, grad_rows, w_in, w_out))
    slot_out = from_experts(produced)
    slot_in_grad = from_experts(back)
    key_grad = jnp.zeros(slot_keys.shape, jnp.float32)
    grads = []
    for clip_index in range(clip_count):
        disp_prob = disp_list[clip_index]
        comb_prob = comb_list[clip_index]
        comb_back = jnp.dot(out_grad[clip_index], slot_out[clip_index].T, preferred_element_type=jnp.float32)
        disp_back = jnp.dot(tokens[clip_index], slot_in_grad[clip_index].T, preferred_element_type=jnp.float32)
        disp_part = disp_prob * (disp_back - jnp.sum(disp_prob * disp_back, axis=0, keepdims=True))
        comb_part = comb_prob * (comb_back - jnp.sum(comb_prob * comb_back, axis=1, keepdims=True))
        logit_grad = (disp_part + comb_part).astype(jnp.bfloat16)
        token_grad = jnp.dot(logit_grad, slot_keys.T, preferred_element_type=jnp.float32) + jnp.dot(disp_prob.astype(jnp.bfloat16), slot_in_grad[clip_index], preferred_element_type=jnp.float32)
        grads.append(token_grad.astype(jnp.bfloat16))
        key_grad = key_grad + jnp.dot(tokens[clip_index].T, logit_grad, preferred_element_type=jnp.float32)
    return jnp.stack(grads), key_grad, w_in_grad, w_out_grad
```

```python
import jax
import jax.numpy as jnp
from jax import lax
from jax.experimental import pallas as pl
from jax.experimental.pallas import tpu as pltpu
from jax.sharding import PartitionSpec as P

MESH = pl.DeviceIdType.MESH
BF = jnp.bfloat16
F32 = jnp.float32

T = 640
D = 1024
S = 256
HL = 512
NZ = 8
SIDE = 4
NC = SIDE * SIDE

GELU_A = 0.7978845608028654
GELU_B = 0.044715


def gelu_value(value):
    return 0.5 * value * (1.0 + jnp.tanh(GELU_A * (value + GELU_B * value * value * value)))


def gelu_slope(value):
    inner = jnp.tanh(GELU_A * (value + GELU_B * value * value * value))
    return 0.5 * (1.0 + inner) + 0.5 * value * (1.0 - inner * inner) * GELU_A * (
        1.0 + 3.0 * GELU_B * value * value
    )


def nn(a, b):
    return lax.dot_general(a, b, (((1,), (0,)), ((), ())), preferred_element_type=F32)


def nt(a, b):
    return lax.dot_general(a, b, (((1,), (1,)), ((), ())), preferred_element_type=F32)


def tn(a, b):
    return lax.dot_general(a, b, (((0,), (0,)), ((), ())), preferred_element_type=F32)


def fold(rows):
    return jnp.concatenate([rows[:, : D // 2], rows[:, D // 2 :]], axis=0)


def unfold(rows):
    return jnp.concatenate([rows[:8], rows[8:]], axis=1)


def lanes(shape, columns):
    at = lax.broadcasted_iota(jnp.int32, shape, 1)
    tile = jnp.zeros(shape, F32)
    for i, column in enumerate(columns):
        tile = jnp.where(at == i, column, tile)
    return tile


def split2(value):
    high = value.astype(BF).astype(F32)
    return high, value - high


def kernel(
    x_hbm, keys_hbm, wi_hbm, wo_hbm, g_hbm,
    tg_hbm, kg_hbm, wig_hbm, wog_hbm,
    x, keys, wi, wo, g,
    keysT, LT, comb, combH, disp, xT,
    gs_send, gs_recv, gsum, gpk, garr,
    us_send, us_recv, usum, ustat, upk, uarr,
    rown, zg, zu, gall, rall, pre, act, pg, outp,
    cpk, crecv, bpk, brecv,
    so, si, sof, sif, cpart, lgH, lgN, dispH,
    ks_send, ks_recv, ksum, kpk, karr, kz, kzarr, kout,
    tgs, wigs, wogs,
    ld, st, sib_s, sib_r,
    ag_s, ag_r, au_s, au_r,
    bg_s, bg_r, bu_s, bu_r,
    co_s, co_r, cb_s, cb_r,
    do_s, do_r, db_s, db_r, fo_s, fo_r, fb_s, fb_r,
    fk_s, fk_r, fz_s, fz_r,
):
    dp = lax.axis_index("dp")
    ctx = lax.axis_index("ctx")
    core = lax.rem(ctx, 2)
    chip = lax.div(ctx, 2)
    cy, cx = lax.div(chip, SIDE), lax.rem(chip, SIDE)
    other = 1 - core
    sib = {"ctx": chip * 2 + other}

    def ahead(d):
        return lax.rem(cy + lax.div(d, SIDE), SIDE) * SIDE + lax.rem(cx + lax.rem(d, SIDE), SIDE)

    def behind(d):
        return (
            lax.rem(cy + SIDE - lax.div(d, SIDE), SIDE) * SIDE
            + lax.rem(cx + SIDE - lax.rem(d, SIDE), SIDE)
        )

    def zahead(e):
        return lax.rem(dp + e, NZ)

    def zbehind(e):
        return lax.rem(dp + NZ - e, NZ)

    def loop(lo, hi, body):
        def step(i, carry):
            body(i)
            return carry

        lax.fori_loop(lo, hi, step, 0)

    def remote(src, dst, send, recv, device):
        return pltpu.make_async_remote_copy(
            src_ref=src, dst_ref=dst, send_sem=send, recv_sem=recv,
            device_id=device, device_id_type=MESH,
        )

    load_keys = pltpu.make_async_copy(keys_hbm, keys, ld.at[0])
    load_x = pltpu.make_async_copy(x_hbm, x, ld.at[1])
    load_g = pltpu.make_async_copy(g_hbm, g, ld.at[2])
    load_wo = pltpu.make_async_copy(wo_hbm, wo, ld.at[3])
    load_wi = pltpu.make_async_copy(wi_hbm, wi, ld.at[4])
    for copy in (load_keys, load_x, load_g, load_wo, load_wi):
        copy.start()

    barrier = pltpu.get_barrier_semaphore()
    pl.semaphore_signal(barrier, inc=1, device_id=sib, device_id_type=MESH)

    def greet_plane(d):
        pl.semaphore_signal(
            barrier, inc=1, device_id={"ctx": ahead(d) * 2 + core}, device_id_type=MESH
        )

    loop(1, NC, greet_plane)

    def greet_z(e):
        pl.semaphore_signal(barrier, inc=1, device_id={"dp": zahead(e)}, device_id_type=MESH)

    loop(1, NZ, greet_z)

    load_keys.wait()
    for b in range(D // 128):
        block = keys[b * 128 : (b + 1) * 128, :].astype(F32).T
        keysT[:, b * 128 : (b + 1) * 128] = jnp.concatenate(
            [block[(2 * j + k) * 8 : (2 * j + k) * 8 + 8] for k in range(2) for j in range(NC)], axis=0
        ).astype(BF)
    load_x.wait()
    LT[...] = nt(keysT[...], x[...])
    for t in range(T // 128):
        at = slice(t * 128, (t + 1) * 128)
        logit = LT[:, at]
        e = jnp.exp(logit - jnp.max(logit, axis=0, keepdims=True))
        e = e / jnp.sum(e, axis=0, keepdims=True)
        comb[:, at] = e
        combH[:, at] = e.astype(BF)
    load_g.wait()
    mine = pl.ds(pl.multiple_of(core * 128, 128), 128)
    theirs = pl.ds(pl.multiple_of(other * 128, 128), 128)
    gs_send[...] = nn(combH[theirs, :], g[...]).astype(BF)
    pl.semaphore_wait(barrier, NC + NZ - 1)
    sib_g = remote(gs_send, gs_recv, sib_s.at[0], sib_r.at[0], sib)
    sib_g.start()
    gsum[...] = nn(combH[mine, :], g[...])

    logit = LT[...]
    top = jnp.max(logit, axis=1, keepdims=True).astype(BF).astype(F32)
    e = jnp.exp(logit - top)
    total = jnp.sum(e, axis=1, keepdims=True)
    disp[...] = e.astype(BF)
    high, low = split2(total)
    ustat[...] = lanes((S, 128), (top, high, low))
    us_send[:, :D] = nn(disp[theirs, :], x[...]).astype(BF)
    us_send[:, D:] = ustat[theirs, :].astype(BF)
    sib_u = remote(us_send, us_recv, sib_s.at[1], sib_r.at[1], sib)
    sib_u.start()

    sib_g.wait_recv()
    gsum[...] += gs_recv[...].astype(F32)

    def ag(d):
        j = ahead(d)
        return remote(gpk.at[j], garr.at[d], ag_s.at[d], ag_r.at[d], {"ctx": j * 2 + core})

    def send_g(d):
        j = ahead(d)
        gpk[j] = fold(gsum[pl.ds(pl.multiple_of(j * 8, 8), 8), :]).astype(BF)
        ag(d).start()

    loop(1, NC, send_g)

    usum[...] = nn(disp[mine, :], x[...])
    own = ustat[mine, :]
    sib_u.wait_recv()
    got = us_recv[:, D:].astype(F32)
    top_a, top_b = own[:, 0:1], got[:, 0:1]
    top = jnp.maximum(top_a, top_b)
    wa, wb = jnp.exp(top_a - top), jnp.exp(top_b - top)
    total = (own[:, 1:2] + own[:, 2:3]) * wa + (got[:, 1:2] + got[:, 2:3]) * wb
    usum[...] = usum[...] * wa + us_recv[:, :D].astype(F32) * wb
    high, low = split2(total)
    ustat[0:128, :] = lanes((128, 128), (top, high, low))

    def pack_u(j):
        at = pl.ds(pl.multiple_of(j * 8, 8), 8)
        s = ustat[at, :]
        return jnp.concatenate([fold(usum[at, :]), jnp.concatenate([s, s], axis=0)], axis=1)

    def au(d):
        j = ahead(d)
        return remote(upk.at[j], uarr.at[d], au_s.at[d], au_r.at[d], {"ctx": j * 2 + core})

    def send_u(d):
        j = ahead(d)
        upk[j] = pack_u(j).astype(BF)
        au(d).start()

    loop(1, NC, send_u)

    for b in range(D // 128):
        block = x[:, b * 128 : (b + 1) * 128].astype(F32).T.astype(BF)
        xT[0, b * 64 : (b + 1) * 64, :] = jnp.concatenate([block[0:32], block[64:96]], axis=0)
        xT[1, b * 64 : (b + 1) * 64, :] = jnp.concatenate([block[32:64], block[96:128]], axis=0)

    def add_g(d, acc):
        ag(d).wait_recv()
        return acc + garr[d].astype(F32)

    acc = fold(gsum[pl.ds(pl.multiple_of(chip * 8, 8), 8), :])
    zg[dp] = lax.fori_loop(1, NC, add_g, acc).astype(BF)

    def bg(e):
        return remote(zg.at[dp], zg.at[dp], bg_s.at[e], bg_r.at[e], {"dp": zahead(e)})

    def bg_in(e):
        j = zbehind(e)
        return remote(zg.at[j], zg.at[j], bg_s.at[e], bg_r.at[e], {"dp": zahead(e)})

    loop(1, NZ, lambda e: bg(e).start())

    uarr[0] = pack_u(chip).astype(BF)
    half = D // 2

    def top_u(d, top):
        au(d).wait_recv()
        return jnp.maximum(top, uarr[d, :, half : half + 128].astype(F32))

    tops = lax.fori_loop(1, NC, top_u, uarr[0, :, half : half + 128].astype(F32))
    top = tops[:, 0:1]

    def add_u(d, carry):
        acc, total = carry
        piece = uarr[d].astype(F32)
        w = jnp.exp(piece[:, half : half + 1] - top)
        total = total + w * (piece[:, half + 1 : half + 2] + piece[:, half + 2 : half + 3])
        return acc + w * piece[:, :half], total

    acc, total = lax.fori_loop(
        0, NC, add_u, (jnp.zeros((16, half), F32), jnp.zeros((16, 1), F32))
    )
    acc = acc / total
    rown[...] = acc
    zu[dp] = acc.astype(BF)

    def bu(e):
        return remote(zu.at[dp], zu.at[dp], bu_s.at[e], bu_r.at[e], {"dp": zahead(e)})

    def bu_in(e):
        j = zbehind(e)
        return remote(zu.at[j], zu.at[j], bu_s.at[e], bu_r.at[e], {"dp": zahead(e)})

    loop(1, NZ, lambda e: bu(e).start())

    first = lax.rem(lax.broadcasted_iota(jnp.int32, (64, HL), 0), 8) < 4
    loop(1, NZ, lambda e: bg_in(e).wait_recv())
    gall[...] = jnp.concatenate([unfold(zg[c].astype(F32)) for c in range(NZ)], axis=0).astype(BF)
    load_wo.wait()
    act_grad = jnp.where(first, nt(gall[...], wo[0]), nt(gall[...], wo[1]))
    pre[...] = act_grad
    loop(1, NZ, lambda e: bu_in(e).wait_recv())
    rall[...] = jnp.concatenate([unfold(zu[c].astype(F32)) for c in range(NZ)], axis=0).astype(BF)
    load_wi.wait()
    pre_act = jnp.where(first, nn(rall[...], wi[0]), nn(rall[...], wi[1]))
    a = gelu_value(pre_act)
    act[0] = jnp.where(first, a, 0.0).astype(BF)
    act[1] = jnp.where(first, 0.0, a).astype(BF)
    p = pre[...] * gelu_slope(pre_act)
    pg[0] = jnp.where(first, p, 0.0).astype(BF)
    pg[1] = jnp.where(first, 0.0, p).astype(BF)

    def co(e):
        j = zahead(e)
        return remote(cpk.at[j], crecv.at[e], co_s.at[e], co_r.at[e], {"dp": j})

    def cb(e):
        j = zahead(e)
        return remote(bpk.at[j], brecv.at[e], cb_s.at[e], cb_r.at[e], {"dp": j})

    def clip_rows(j):
        return fold(outp[pl.ds(pl.multiple_of(j * 8, 8), 8), :])

    def send_o(e):
        j = zahead(e)
        cpk[j] = clip_rows(j).astype(BF)
        co(e).start()

    outp[...] = nn(act[0], wo[0]) + nn(act[1], wo[1])
    loop(1, NZ, send_o)
    o_own = clip_rows(dp)

    def send_b(e):
        j = zahead(e)
        bpk[j] = clip_rows(j).astype(BF)
        cb(e).start()

    outp[...] = nt(pg[0], wi[0]) + nt(pg[1], wi[1])
    loop(1, NZ, send_b)
    b_own = clip_rows(dp)

    for e in range(2):
        for c in range(HL // 128):
            at = slice(c * 128, (c + 1) * 128)
            wogs[e, at, :] = tn(act[e, :, at], gall[...]).astype(BF)
    store_wo = pltpu.make_async_copy(wogs, wog_hbm, st.at[0])
    store_wo.start()

    def add_o(e, acc):
        co(e).wait_recv()
        return acc + crecv[e].astype(F32)

    so[core, chip] = lax.fori_loop(1, NZ, add_o, o_own).astype(BF)

    def do(d):
        return remote(
            so.at[core, chip], so.at[core, chip], do_s.at[d], do_r.at[d], {"ctx": ahead(d) * 2 + core}
        )

    def fo(d):
        j = behind(d)
        return remote(so.at[core, j], so.at[core, j], fo_s.at[d], fo_r.at[d], sib)

    loop(1, NC, lambda d: do(d).start())
    fo(0).start()

    def add_b(e, acc):
        cb(e).wait_recv()
        return acc + brecv[e].astype(F32)

    back = lax.fori_loop(1, NZ, add_b, b_own).astype(BF)
    si[core, chip, :, :half] = back
    inner = jnp.sum(rown[...] * back.astype(F32), axis=1, keepdims=True)
    inner = inner[:8] + inner[8:]
    inner = jnp.concatenate([inner, inner], axis=0)
    z_high, z_low = split2(total)
    i_high, i_low = split2(inner)
    si[core, chip, :, half:] = lanes((16, 128), (top, z_high, z_low, i_high, i_low)).astype(BF)

    def db(d):
        return remote(
            si.at[core, chip], si.at[core, chip], db_s.at[d], db_r.at[d], {"ctx": ahead(d) * 2 + core}
        )

    def fb(d):
        j = behind(d)
        return remote(si.at[core, j], si.at[core, j], fb_s.at[d], fb_r.at[d], sib)

    loop(1, NC, lambda d: db(d).start())
    fb(0).start()

    def pass_o(d):
        do(d).wait_recv()
        fo(d).start()

    loop(1, NC, pass_o)

    def pass_b(d):
        db(d).wait_recv()
        fb(d).start()

    for e in range(2):
        for c in range(D // 128):
            at = slice(c * 128, (c + 1) * 128)
            wigs[e, at, :] = tn(rall[:, at], pg[e]).astype(BF)
    store_wi = pltpu.make_async_copy(wigs, wig_hbm, st.at[1])
    store_wi.start()

    loop(1, NC, pass_b)
    loop(0, NC, lambda d: fo(d).wait_recv())

    def rows_of(ref, k, q):
        return jnp.concatenate(
            [unfold(ref[k, 2 * q, :, :half].astype(F32)), unfold(ref[k, 2 * q + 1, :, :half].astype(F32))],
            axis=0,
        ).astype(BF)

    for k in range(2):
        for q in range(NC // 2):
            at = k * 128 + q * 16
            sof[at : at + 16, :] = rows_of(so, k, q)
    cpart[...] = nt(sof[...], g[...])
    for t in range(T // 128):
        at = slice(t * 128, (t + 1) * 128)
        prob, back = comb[:, at], cpart[:, at]
        cpart[:, at] = prob * (back - jnp.sum(prob * back, axis=0, keepdims=True))

    loop(0, NC, lambda d: fb(d).wait_recv())
    for k in range(2):
        for q in range(NC // 2):
            at = k * 128 + q * 16
            sif[at : at + 16, :] = rows_of(si, k, q)
    stat = jnp.concatenate(
        [si[k, j, 0:8, half : half + 128].astype(F32) for k in range(2) for j in range(NC)], axis=0
    )
    top = stat[:, 0:1]
    over = 1.0 / (stat[:, 1:2] + stat[:, 2:3])
    inner = stat[:, 3:4] + stat[:, 4:5]
    comb[...] = nt(sif[...], x[...])
    for t in range(T // 128):
        at = slice(t * 128, (t + 1) * 128)
        prob = jnp.exp(LT[:, at] - top) * over
        dispH[:, at] = prob.astype(BF)
        lg = prob * (comb[:, at] - inner) + cpart[:, at]
        lgH[:, at] = lg.astype(BF)
        lgN[:, at] = jnp.concatenate(
            [lg[k * 128 + j * 8 : k * 128 + j * 8 + 8] for j in range(NC) for k in range(2)], axis=0
        ).astype(BF)

    ks_send[...] = nt(xT[other], lgN[...]).astype(BF)
    sib_k = remote(ks_send, ks_recv, sib_s.at[2], sib_r.at[2], sib)
    sib_k.start()
    ksum[...] = nt(xT[core], lgN[...])
    sib_k.wait_recv()
    ksum[...] += ks_recv[...].astype(F32)

    def fk(d):
        j = ahead(d)
        return remote(kpk.at[j], karr.at[d], fk_s.at[d], fk_r.at[d], {"ctx": j * 2 + core})

    def key_rows(j):
        return ksum[pl.ds(pl.multiple_of(j * 32, 32), 32), :]

    def send_k(d):
        j = ahead(d)
        kpk[j] = key_rows(j).astype(BF)
        fk(d).start()

    loop(1, NC, send_k)

    for t in range(T // 128):
        at = slice(t * 128, (t + 1) * 128)
        tgs[at, :] = (tn(lgH[:, at], keysT[...]) + tn(dispH[:, at], sif[...])).astype(BF)
    store_tg = pltpu.make_async_copy(tgs, tg_hbm, st.at[2])
    store_tg.start()

    def add_k(d, acc):
        fk(d).wait_recv()
        return acc + karr[d].astype(F32)

    acc = lax.fori_loop(1, NC, add_k, key_rows(chip))
    kz[...] = acc.astype(BF)

    def fz(e):
        return remote(kz, kzarr.at[e], fz_s.at[e], fz_r.at[e], {"dp": zahead(e)})

    loop(1, NZ, lambda e: fz(e).start())

    def add_z(e, acc):
        fz(e).wait_recv()
        return acc + kzarr[e].astype(F32)

    kout[...] = lax.fori_loop(1, NZ, add_z, acc)
    store_kg = pltpu.make_async_copy(kout, kg_hbm, st.at[3])
    store_kg.start()

    sib_g.wait_send()
    sib_u.wait_send()
    sib_k.wait_send()

    def drain_plane(d):
        ag(d).wait_send()
        au(d).wait_send()
        do(d).wait_send()
        db(d).wait_send()
        fk(d).wait_send()

    loop(1, NC, drain_plane)

    def drain_pass(d):
        fo(d).wait_send()
        fb(d).wait_send()

    loop(0, NC, drain_pass)

    def drain_z(e):
        bg(e).wait_send()
        bu(e).wait_send()
        co(e).wait_send()
        cb(e).wait_send()
        fz(e).wait_send()

    loop(1, NZ, drain_z)
    store_wo.wait()
    store_wi.wait()
    store_tg.wait()
    store_kg.wait()


def per_device(tokens, slot_keys, w_in, w_out, out_grad):
    hbm = pl.BlockSpec(memory_space=pl.ANY)
    vmem = pltpu.VMEM
    half = D // 2
    plane, line = pltpu.SemaphoreType.DMA((NC,)), pltpu.SemaphoreType.DMA((NZ,))
    tg, kg, wig, wog = pl.pallas_call(
        kernel,
        out_shape=(
            jax.ShapeDtypeStruct((T, D), BF),
            jax.ShapeDtypeStruct((32, S), F32),
            jax.ShapeDtypeStruct((2, D, HL), BF),
            jax.ShapeDtypeStruct((2, HL, D), BF),
        ),
        in_specs=[hbm] * 5,
        out_specs=(hbm,) * 4,
        scratch_shapes=[
            vmem((T, D), BF), vmem((D, S), BF), vmem((2, D, HL), BF), vmem((2, HL, D), BF), vmem((T, D), BF),
            vmem((S, D), BF), vmem((S, T), F32), vmem((S, T), F32), vmem((S, T), BF), vmem((S, T), BF),
            vmem((2, D // 2, T), BF),
            vmem((128, D), BF), vmem((128, D), BF), vmem((128, D), F32),
            vmem((NC, 16, half), BF), vmem((NC, 16, half), BF),
            vmem((128, D + 128), BF), vmem((128, D + 128), BF), vmem((128, D), F32), vmem((S, 128), F32),
            vmem((NC, 16, half + 128), BF), vmem((NC, 16, half + 128), BF),
            vmem((16, half), F32), vmem((NZ, 16, half), BF), vmem((NZ, 16, half), BF),
            vmem((64, D), BF), vmem((64, D), BF), vmem((64, HL), F32),
            vmem((2, 64, HL), BF), vmem((2, 64, HL), BF), vmem((64, D), F32),
            vmem((NZ, 16, half), BF), vmem((NZ, 16, half), BF),
            vmem((NZ, 16, half), BF), vmem((NZ, 16, half), BF),
            vmem((2, NC, 16, half), BF), vmem((2, NC, 16, half + 128), BF), vmem((S, D), BF), vmem((S, D), BF),
            vmem((S, T), F32), vmem((S, T), BF), vmem((S, T), BF), vmem((S, T), BF),
            vmem((D // 2, S), BF), vmem((D // 2, S), BF), vmem((D // 2, S), F32),
            vmem((NC, 32, S), BF), vmem((NC, 32, S), BF), vmem((32, S), BF), vmem((NZ, 32, S), BF),
            vmem((32, S), F32),
            vmem((T, D), BF), vmem((2, D, HL), BF), vmem((2, HL, D), BF),
            pltpu.SemaphoreType.DMA((5,)), pltpu.SemaphoreType.DMA((4,)),
            pltpu.SemaphoreType.DMA((3,)), pltpu.SemaphoreType.DMA((3,)),
            plane, plane, plane, plane,
            line, line, line, line,
            line, line, line, line,
            plane, plane, plane, plane, plane, plane, plane, plane,
            plane, plane, line, line,
        ],
        compiler_params=pltpu.CompilerParams(
            collective_id=0, has_side_effects=True, vmem_limit_bytes=60 * 2**20
        ),
        cost_estimate=pl.CostEstimate(flops=4 * 10**9, bytes_accessed=13 * 10**6, transcendentals=10**6),
    )(tokens[0], slot_keys, w_in, w_out, out_grad[0])
    return tg[None], kg, wig, wog


def solution(mesh):
    return jax.shard_map(
        per_device,
        mesh=mesh,
        in_specs=(
            P("dp", "ctx", None),
            P(),
            P("ctx", None, "dp"),
            P("ctx", "dp", None),
            P("dp", "ctx", None),
        ),
        out_specs=(
            P("dp", "ctx", None),
            P("ctx", None),
            P("ctx", None, "dp"),
            P("ctx", "dp", None),
        ),
        check_vma=False,
    )
```

```python
import jax
import jax.numpy as jnp
from jax import lax
from jax.experimental import pallas as pl
from jax.experimental.pallas import tpu as pltpu
from jax.sharding import PartitionSpec as P

MESH = pl.DeviceIdType.MESH
BF = jnp.bfloat16
F32 = jnp.float32

T = 640
D = 1024
S = 256
HL = 512
NZ = 8
SIDE = 4
NC = SIDE * SIDE

PLANE = sorted(range(1, NC), key=lambda d: -sum(min(i, SIDE - i) for i in divmod(d, SIDE)))
LINE = sorted(range(1, NZ), key=lambda e: -min(e, NZ - e))

GELU_A = 0.7978845608028654
GELU_B = 0.044715


def gelu_value(value):
    return 0.5 * value * (1.0 + jnp.tanh(GELU_A * (value + GELU_B * value * value * value)))


def gelu_slope(value):
    inner = jnp.tanh(GELU_A * (value + GELU_B * value * value * value))
    return 0.5 * (1.0 + inner) + 0.5 * value * (1.0 - inner * inner) * GELU_A * (
        1.0 + 3.0 * GELU_B * value * value
    )


def nn(a, b):
    return lax.dot_general(a, b, (((1,), (0,)), ((), ())), preferred_element_type=F32)


def nt(a, b):
    return lax.dot_general(a, b, (((1,), (1,)), ((), ())), preferred_element_type=F32)


def tn(a, b):
    return lax.dot_general(a, b, (((0,), (0,)), ((), ())), preferred_element_type=F32)


def fold(rows):
    return jnp.concatenate([rows[:, : D // 2], rows[:, D // 2 :]], axis=0)


def unfold(rows):
    return jnp.concatenate([rows[:8], rows[8:]], axis=1)


def add_all(acc, ref, n):
    for i in range(1, n):
        acc = acc + ref[i].astype(F32)
    return acc


def lanes(shape, columns):
    at = lax.broadcasted_iota(jnp.int32, shape, 1)
    tile = jnp.zeros(shape, F32)
    for i, column in enumerate(columns):
        tile = jnp.where(at == i, column, tile)
    return tile


def split2(value):
    high = value.astype(BF).astype(F32)
    return high, value - high


class Copies:
    def __init__(self, open_copies, make, low, high):
        self.make, self.low, self.high = make, low, high
        self.order = {NC: PLANE, NZ: LINE}.get(high, [0])
        self.sent = self.received = True
        open_copies.append(self)

    def start(self, d):
        self.sent = self.received = False
        self.make(d).start()

    def start_all(self):
        for d in self.order:
            self.start(d)

    def wait_recv(self, d):
        self.received = True
        self.make(d).wait_recv()

    def wait_recv_all(self):
        loop(self.low, self.high, self.wait_recv)

    def wait_send(self, d):
        self.make(d).wait_send()

    def drain(self):
        if not self.received:
            self.wait_recv_all()
        if not self.sent:
            loop(self.low, self.high, self.wait_send)


class Local:
    def __init__(self, open_copies, *copy):
        self.copy = pltpu.make_async_copy(*copy)
        self.waited = True
        open_copies.append(self)

    def start(self):
        self.waited = False
        self.copy.start()

    def wait(self):
        self.waited = True
        self.copy.wait()

    def drain(self):
        if not self.waited:
            self.wait()


def loop(low, high, body):
    def step(i, carry):
        body(i)
        return carry

    lax.fori_loop(low, high, step, 0)


def kernel(
    x_hbm, keys_hbm, wi_hbm, wo_hbm, g_hbm,
    tgs, kout, wigs, wogs,
    x, keys, wi, wo, g,
    keysT, LT, comb, combH, disp, xT,
    gs_send, gs_recv, gsum, gpk, garr,
    us_send, us_recv, usum, ustat, upk, uarr,
    rown, zg, zu, gall, rall, pre, act, pg, outp,
    cpk, crecv, bpk, brecv,
    so, si, sof, sif, cpart, lgH, lgN, dispH,
    ks_send, ks_recv, ksum, kpk, karr, kz, kzarr,
    ld, sib_s, sib_r,
    ag_s, ag_r, au_s, au_r,
    bg_s, bg_r, bu_s, bu_r,
    co_s, co_r, cb_s, cb_r,
    do_s, do_r, db_s, db_r, fo_s, fo_r, fb_s, fb_r,
    fk_s, fk_r, fz_s, fz_r,
):
    dp = lax.axis_index("dp")
    ctx = lax.axis_index("ctx")
    core = lax.rem(ctx, 2)
    chip = lax.div(ctx, 2)
    cy, cx = lax.div(chip, SIDE), lax.rem(chip, SIDE)
    other = 1 - core
    sib = {"ctx": chip * 2 + other}

    def ahead(d):
        return lax.rem(cy + d // SIDE, SIDE) * SIDE + lax.rem(cx + d % SIDE, SIDE)

    def behind(d):
        return (
            lax.rem(cy + SIDE - d // SIDE, SIDE) * SIDE
            + lax.rem(cx + SIDE - d % SIDE, SIDE)
        )

    def zahead(e):
        return lax.rem(dp + e, NZ)

    def zbehind(e):
        return lax.rem(dp + NZ - e, NZ)

    open_copies = []

    def remote(src, dst, send, recv, device):
        return pltpu.make_async_remote_copy(
            src_ref=src, dst_ref=dst, send_sem=send, recv_sem=recv,
            device_id=device, device_id_type=MESH,
        )

    load_keys = Local(open_copies, keys_hbm, keys, ld.at[0])
    parts = (slice(0, 256), slice(256, 512), slice(512, T))
    load_x = [Local(open_copies, x_hbm.at[at], x.at[at], ld.at[5 + i]) for i, at in enumerate(parts)]
    load_g = Local(open_copies, g_hbm, g, ld.at[2])
    load_wo = Local(open_copies, wo_hbm, wo, ld.at[3])
    load_wi = Local(open_copies, wi_hbm, wi, ld.at[4])
    for copy in (load_keys, *load_x, load_g):
        copy.start()

    barrier = pltpu.get_barrier_semaphore()
    pl.semaphore_signal(barrier, inc=1, device_id=sib, device_id_type=MESH)

    def greet_plane(d):
        pl.semaphore_signal(
            barrier, inc=1, device_id={"ctx": ahead(d) * 2 + core}, device_id_type=MESH
        )

    loop(1, NC, greet_plane)

    def greet_z(e):
        pl.semaphore_signal(barrier, inc=1, device_id={"dp": zahead(e)}, device_id_type=MESH)

    loop(1, NZ, greet_z)

    load_keys.wait()
    for b in range(D // 128):
        block = keys[b * 128 : (b + 1) * 128, :].astype(F32).T
        keysT[:, b * 128 : (b + 1) * 128] = jnp.concatenate(
            [block[(2 * j + k) * 8 : (2 * j + k) * 8 + 8] for k in range(2) for j in range(NC)], axis=0
        ).astype(BF)
    for copy, part in zip(load_x, parts):
        copy.wait()
        LT[:, part] = nt(keysT[...], x[part, :])
        for t in range(part.start // 128, part.stop // 128):
            at = slice(t * 128, (t + 1) * 128)
            logit = LT[:, at]
            e = jnp.exp(logit - jnp.max(logit, axis=0, keepdims=True))
            e = e / jnp.sum(e, axis=0, keepdims=True)
            comb[:, at] = e
            combH[:, at] = e.astype(BF)
    load_g.wait()
    mine = pl.ds(pl.multiple_of(core * 128, 128), 128)
    theirs = pl.ds(pl.multiple_of(other * 128, 128), 128)
    gs_send[...] = nn(combH[theirs, :], g[...]).astype(BF)
    pl.semaphore_wait(barrier, NC + NZ - 1)
    sib_g = Copies(open_copies, lambda d: remote(gs_send, gs_recv, sib_s.at[0], sib_r.at[0], sib), 0, 1)
    sib_g.start(0)
    load_wo.start()
    load_wi.start()

    logit = LT[...]
    top = jnp.max(logit, axis=1, keepdims=True).astype(BF).astype(F32)
    e = jnp.exp(logit - top)
    total = jnp.sum(e, axis=1, keepdims=True)
    disp[...] = e.astype(BF)
    high, low = split2(total)
    ustat[...] = lanes((S, 128), (top, high, low))
    us_send[:, :D] = nn(disp[theirs, :], x[...]).astype(BF)
    us_send[:, D:] = ustat[theirs, :].astype(BF)
    sib_u = Copies(open_copies, lambda d: remote(us_send, us_recv, sib_s.at[1], sib_r.at[1], sib), 0, 1)
    sib_u.start(0)
    gsum[...] = nn(combH[mine, :], g[...])
    usum[...] = nn(disp[mine, :], x[...])

    sib_g.wait_recv(0)
    gsum[...] += gs_recv[...].astype(F32)

    def ag_copy(d):
        j = ahead(d)
        return remote(gpk.at[j], garr.at[d], ag_s.at[d], ag_r.at[d], {"ctx": j * 2 + core})

    ag = Copies(open_copies, ag_copy, 1, NC)

    def send_g(d):
        j = ahead(d)
        gpk[j] = fold(gsum[pl.ds(pl.multiple_of(j * 8, 8), 8), :]).astype(BF)
        ag.start(d)

    for d in PLANE:
        send_g(d)

    own = ustat[mine, :]
    sib_u.wait_recv(0)
    got = us_recv[:, D:].astype(F32)
    top_a, top_b = own[:, 0:1], got[:, 0:1]
    top = jnp.maximum(top_a, top_b)
    wa, wb = jnp.exp(top_a - top), jnp.exp(top_b - top)
    total = (own[:, 1:2] + own[:, 2:3]) * wa + (got[:, 1:2] + got[:, 2:3]) * wb
    usum[...] = usum[...] * wa + us_recv[:, :D].astype(F32) * wb
    high, low = split2(total)
    ustat[0:128, :] = lanes((128, 128), (top, high, low))

    def pack_u(j):
        at = pl.ds(pl.multiple_of(j * 8, 8), 8)
        s = ustat[at, :]
        return jnp.concatenate([fold(usum[at, :]), jnp.concatenate([s, s], axis=0)], axis=1)

    def au_copy(d):
        j = ahead(d)
        return remote(upk.at[j], uarr.at[d], au_s.at[d], au_r.at[d], {"ctx": j * 2 + core})

    au = Copies(open_copies, au_copy, 1, NC)

    def send_u(d):
        j = ahead(d)
        upk[j] = pack_u(j).astype(BF)
        au.start(d)

    for d in PLANE:
        send_u(d)

    for b in range(D // 128):
        block = x[:, b * 128 : (b + 1) * 128].astype(F32).T.astype(BF)
        xT[0, b * 64 : (b + 1) * 64, :] = jnp.concatenate([block[0:32], block[64:96]], axis=0)
        xT[1, b * 64 : (b + 1) * 64, :] = jnp.concatenate([block[32:64], block[96:128]], axis=0)

    acc = fold(gsum[pl.ds(pl.multiple_of(chip * 8, 8), 8), :])
    ag.wait_recv_all()
    zg[dp] = add_all(acc, garr, NC).astype(BF)

    def bg_copy(e):
        return remote(zg.at[dp], zg.at[dp], bg_s.at[e], bg_r.at[e], {"dp": zahead(e)})

    bg = Copies(open_copies, bg_copy, 1, NZ)

    bg.start_all()

    uarr[0] = pack_u(chip).astype(BF)
    half = D // 2

    au.wait_recv_all()
    stats = uarr[:, :, half : half + 128].astype(F32)
    top = jnp.max(stats[:, :, 0:1], axis=0)
    w = jnp.exp(stats[:, :, 0:1] - top)
    total = jnp.sum(w * (stats[:, :, 1:2] + stats[:, :, 2:3]), axis=0)
    acc = jnp.zeros((16, half), F32)
    for d in range(NC):
        acc = acc + w[d] * uarr[d, :, :half].astype(F32)
    acc = acc / total
    rown[...] = acc
    zu[dp] = acc.astype(BF)

    def bu_copy(e):
        return remote(zu.at[dp], zu.at[dp], bu_s.at[e], bu_r.at[e], {"dp": zahead(e)})

    bu = Copies(open_copies, bu_copy, 1, NZ)

    bu.start_all()

    first = lax.rem(lax.broadcasted_iota(jnp.int32, (64, HL), 0), 8) < 4
    bg.wait_recv_all()
    gall[...] = jnp.concatenate([unfold(zg[c].astype(F32)) for c in range(NZ)], axis=0).astype(BF)
    load_wo.wait()
    act_grad = jnp.where(first, nt(gall[...], wo[0]), nt(gall[...], wo[1]))
    pre[...] = act_grad
    bu.wait_recv_all()
    rall[...] = jnp.concatenate([unfold(zu[c].astype(F32)) for c in range(NZ)], axis=0).astype(BF)
    load_wi.wait()
    pre_act = jnp.where(first, nn(rall[...], wi[0]), nn(rall[...], wi[1]))
    a = gelu_value(pre_act)
    act[0] = jnp.where(first, a, 0.0).astype(BF)
    act[1] = jnp.where(first, 0.0, a).astype(BF)
    p = pre[...] * gelu_slope(pre_act)
    pg[0] = jnp.where(first, p, 0.0).astype(BF)
    pg[1] = jnp.where(first, 0.0, p).astype(BF)

    def co_copy(e):
        j = zahead(e)
        return remote(cpk.at[j], crecv.at[e], co_s.at[e], co_r.at[e], {"dp": j})

    co = Copies(open_copies, co_copy, 1, NZ)

    def cb_copy(e):
        j = zahead(e)
        return remote(bpk.at[j], brecv.at[e], cb_s.at[e], cb_r.at[e], {"dp": j})

    cb = Copies(open_copies, cb_copy, 1, NZ)

    def clip_rows(j):
        return fold(outp[pl.ds(pl.multiple_of(j * 8, 8), 8), :])

    def send_o(e):
        j = zahead(e)
        cpk[j] = clip_rows(j).astype(BF)
        co.start(e)

    outp[...] = nn(act[0], wo[0]) + nn(act[1], wo[1])
    for d in LINE:
        send_o(d)
    o_own = clip_rows(dp)

    def send_b(e):
        j = zahead(e)
        bpk[j] = clip_rows(j).astype(BF)
        cb.start(e)

    outp[...] = nt(pg[0], wi[0]) + nt(pg[1], wi[1])
    for d in LINE:
        send_b(d)
    b_own = clip_rows(dp)

    for e in range(2):
        for c in range(HL // 128):
            at = slice(c * 128, (c + 1) * 128)
            wogs[e, at, :] = tn(act[e, :, at], gall[...]).astype(BF)

    co.wait_recv_all()
    so[core, chip] = add_all(o_own, crecv, NZ).astype(BF)

    def do_copy(d):
        return remote(
            so.at[core, chip], so.at[core, chip], do_s.at[d], do_r.at[d], {"ctx": ahead(d) * 2 + core}
        )

    do = Copies(open_copies, do_copy, 1, NC)

    def fo_copy(d):
        j = behind(d)
        return remote(so.at[core, j], so.at[core, j], fo_s.at[d], fo_r.at[d], sib)

    fo = Copies(open_copies, fo_copy, 0, NC)


    do.start_all()
    fo.start(0)

    cb.wait_recv_all()
    back = add_all(b_own, brecv, NZ).astype(BF)
    si[core, chip, :, :half] = back
    inner = jnp.sum(rown[...] * back.astype(F32), axis=1, keepdims=True)
    inner = inner[:8] + inner[8:]
    inner = jnp.concatenate([inner, inner], axis=0)
    z_high, z_low = split2(total)
    i_high, i_low = split2(inner)
    si[core, chip, :, half:] = lanes((16, 128), (top, z_high, z_low, i_high, i_low)).astype(BF)

    def db_copy(d):
        return remote(
            si.at[core, chip], si.at[core, chip], db_s.at[d], db_r.at[d], {"ctx": ahead(d) * 2 + core}
        )

    db = Copies(open_copies, db_copy, 1, NC)

    def fb_copy(d):
        j = behind(d)
        return remote(si.at[core, j], si.at[core, j], fb_s.at[d], fb_r.at[d], sib)

    fb = Copies(open_copies, fb_copy, 0, NC)


    db.start_all()
    fb.start(0)

    def pass_o(d):
        do.wait_recv(d)
        fo.start(d)

    loop(1, NC, pass_o)

    def pass_b(d):
        db.wait_recv(d)
        fb.start(d)

    for e in range(2):
        for c in range(D // 128):
            at = slice(c * 128, (c + 1) * 128)
            wigs[e, at, :] = tn(rall[:, at], pg[e]).astype(BF)

    loop(1, NC, pass_b)
    fo.wait_recv_all()

    def rows_of(ref, k, q):
        return jnp.concatenate(
            [unfold(ref[k, 2 * q, :, :half].astype(F32)), unfold(ref[k, 2 * q + 1, :, :half].astype(F32))],
            axis=0,
        ).astype(BF)

    for k in range(2):
        for q in range(NC // 2):
            at = k * 128 + q * 16
            sof[at : at + 16, :] = rows_of(so, k, q)
    cpart[...] = nt(sof[...], g[...])
    for t in range(T // 128):
        at = slice(t * 128, (t + 1) * 128)
        prob, back = comb[:, at], cpart[:, at]
        cpart[:, at] = prob * (back - jnp.sum(prob * back, axis=0, keepdims=True))

    fb.wait_recv_all()
    for k in range(2):
        for q in range(NC // 2):
            at = k * 128 + q * 16
            sif[at : at + 16, :] = rows_of(si, k, q)
    stat = jnp.concatenate(
        [si[k, j, 0:8, half : half + 128].astype(F32) for k in range(2) for j in range(NC)], axis=0
    )
    top = stat[:, 0:1]
    over = 1.0 / (stat[:, 1:2] + stat[:, 2:3])
    inner = stat[:, 3:4] + stat[:, 4:5]
    comb[...] = nt(sif[...], x[...])
    for t in range(T // 128):
        at = slice(t * 128, (t + 1) * 128)
        prob = jnp.exp(LT[:, at] - top) * over
        dispH[:, at] = prob.astype(BF)
        lg = prob * (comb[:, at] - inner) + cpart[:, at]
        lgH[:, at] = lg.astype(BF)
        lgN[:, at] = jnp.concatenate(
            [lg[k * 128 + j * 8 : k * 128 + j * 8 + 8] for j in range(NC) for k in range(2)], axis=0
        ).astype(BF)

    ks_send[...] = nt(xT[other], lgN[...]).astype(BF)
    sib_k = Copies(open_copies, lambda d: remote(ks_send, ks_recv, sib_s.at[2], sib_r.at[2], sib), 0, 1)
    sib_k.start(0)
    ksum[...] = nt(xT[core], lgN[...])
    sib_k.wait_recv(0)
    ksum[...] += ks_recv[...].astype(F32)

    def fk_copy(d):
        j = ahead(d)
        return remote(kpk.at[j], karr.at[d], fk_s.at[d], fk_r.at[d], {"ctx": j * 2 + core})

    fk = Copies(open_copies, fk_copy, 1, NC)

    def key_rows(j):
        return ksum[pl.ds(pl.multiple_of(j * 32, 32), 32), :]

    def send_k(d):
        j = ahead(d)
        kpk[j] = key_rows(j).astype(BF)
        fk.start(d)

    for d in PLANE:
        send_k(d)

    for t in range(T // 128):
        at = slice(t * 128, (t + 1) * 128)
        tgs[at, :] = (tn(lgH[:, at], keysT[...]) + tn(dispH[:, at], sif[...])).astype(BF)

    fk.wait_recv_all()
    acc = add_all(key_rows(chip), karr, NC)
    kz[...] = acc.astype(BF)

    def fz_copy(e):
        return remote(kz, kzarr.at[e], fz_s.at[e], fz_r.at[e], {"dp": zahead(e)})

    fz = Copies(open_copies, fz_copy, 1, NZ)


    fz.start_all()

    fz.wait_recv_all()
    kout[...] = add_all(acc, kzarr, NZ)

    for copies in open_copies:
        copies.drain()


def store_kernel(tgs, kout, wigs, wogs, tg_hbm, kg_hbm, wig_hbm, wog_hbm, st):
    pairs = ((wigs, wig_hbm), (wogs, wog_hbm), (tgs, tg_hbm), (kout, kg_hbm))
    copies = [pltpu.make_async_copy(src, dst, st.at[i]) for i, (src, dst) in enumerate(pairs)]
    for copy in copies:
        copy.start()
    for copy in copies:
        copy.wait()


def per_device(tokens, slot_keys, w_in, w_out, out_grad):
    hbm = pl.BlockSpec(memory_space=pltpu.HBM)
    vmem = pltpu.VMEM
    half = D // 2
    plane, line = pltpu.SemaphoreType.DMA((NC,)), pltpu.SemaphoreType.DMA((NZ,))
    held = pl.pallas_call(
        kernel,
        out_shape=(
            pltpu.VMEM((T, D), BF),
            pltpu.VMEM((32, S), F32),
            pltpu.VMEM((2, D, HL), BF),
            pltpu.VMEM((2, HL, D), BF),
        ),
        in_specs=[hbm] * 5,
        out_specs=(pl.BlockSpec(memory_space=vmem),) * 4,
        scratch_shapes=[
            vmem((T, D), BF), vmem((D, S), BF), vmem((2, D, HL), BF), vmem((2, HL, D), BF), vmem((T, D), BF),
            vmem((S, D), BF), vmem((S, T), F32), vmem((S, T), F32), vmem((S, T), BF), vmem((S, T), BF),
            vmem((2, D // 2, T), BF),
            vmem((128, D), BF), vmem((128, D), BF), vmem((128, D), F32),
            vmem((NC, 16, half), BF), vmem((NC, 16, half), BF),
            vmem((128, D + 128), BF), vmem((128, D + 128), BF), vmem((128, D), F32), vmem((S, 128), F32),
            vmem((NC, 16, half + 128), BF), vmem((NC, 16, half + 128), BF),
            vmem((16, half), F32), vmem((NZ, 16, half), BF), vmem((NZ, 16, half), BF),
            vmem((64, D), BF), vmem((64, D), BF), vmem((64, HL), F32),
            vmem((2, 64, HL), BF), vmem((2, 64, HL), BF), vmem((64, D), F32),
            vmem((NZ, 16, half), BF), vmem((NZ, 16, half), BF),
            vmem((NZ, 16, half), BF), vmem((NZ, 16, half), BF),
            vmem((2, NC, 16, half), BF), vmem((2, NC, 16, half + 128), BF), vmem((S, D), BF), vmem((S, D), BF),
            vmem((S, T), F32), vmem((S, T), BF), vmem((S, T), BF), vmem((S, T), BF),
            vmem((D // 2, S), BF), vmem((D // 2, S), BF), vmem((D // 2, S), F32),
            vmem((NC, 32, S), BF), vmem((NC, 32, S), BF), vmem((32, S), BF), vmem((NZ, 32, S), BF),
            pltpu.SemaphoreType.DMA((8,)),
            pltpu.SemaphoreType.DMA((3,)), pltpu.SemaphoreType.DMA((3,)),
            plane, plane, plane, plane,
            line, line, line, line,
            line, line, line, line,
            plane, plane, plane, plane, plane, plane, plane, plane,
            plane, plane, line, line,
        ],
        compiler_params=pltpu.CompilerParams(
            collective_id=0, has_side_effects=True, vmem_limit_bytes=36 * 2**20
        ),
        cost_estimate=pl.CostEstimate(flops=4 * 10**9, bytes_accessed=13 * 10**6, transcendentals=10**6),
    )(*(pltpu.with_memory_space_constraint(a, pltpu.HBM) for a in (tokens[0], slot_keys, w_in, w_out, out_grad[0])))
    tg, kg, wig, wog = pl.pallas_call(
        store_kernel,
        out_shape=(
            pltpu.HBM((T, D), BF),
            pltpu.HBM((32, S), F32),
            pltpu.HBM((2, D, HL), BF),
            pltpu.HBM((2, HL, D), BF),
        ),
        in_specs=[pl.BlockSpec(memory_space=vmem)] * 4,
        out_specs=(hbm,) * 4,
        scratch_shapes=[pltpu.SemaphoreType.DMA((4,))],
        compiler_params=pltpu.CompilerParams(vmem_limit_bytes=2**20),
    )(*held)
    return tg[None], kg, wig, wog


def solution(mesh):
    return jax.shard_map(
        per_device,
        mesh=mesh,
        in_specs=(
            P("dp", "ctx", None),
            P(),
            P("ctx", None, "dp"),
            P("ctx", "dp", None),
            P("dp", "ctx", None),
        ),
        out_specs=(
            P("dp", "ctx", None),
            P("ctx", None),
            P("ctx", None, "dp"),
            P("ctx", "dp", None),
        ),
        check_vma=False,
    )
```

```python
import jax
import jax.numpy as jnp
from jax import lax
from jax.experimental import pallas as pl
from jax.experimental.pallas import tpu as pltpu
from jax.sharding import PartitionSpec as P

MESH = pl.DeviceIdType.MESH
BF = jnp.bfloat16
F32 = jnp.float32

T = 640
D = 1024
S = 256
HL = 512
NZ = 8
SIDE = 4
NC = SIDE * SIDE

PLANE = sorted(range(1, NC), key=lambda d: -sum(min(i, SIDE - i) for i in divmod(d, SIDE)))
LINE = sorted(range(1, NZ), key=lambda e: -min(e, NZ - e))

GELU_A = 0.7978845608028654
GELU_B = 0.044715


def gelu_value(value):
    return 0.5 * value * (1.0 + jnp.tanh(GELU_A * (value + GELU_B * value * value * value)))


def gelu_slope(value):
    inner = jnp.tanh(GELU_A * (value + GELU_B * value * value * value))
    return 0.5 * (1.0 + inner) + 0.5 * value * (1.0 - inner * inner) * GELU_A * (
        1.0 + 3.0 * GELU_B * value * value
    )


def nn(a, b):
    return lax.dot_general(a, b, (((1,), (0,)), ((), ())), preferred_element_type=F32)


def nt(a, b):
    return lax.dot_general(a, b, (((1,), (1,)), ((), ())), preferred_element_type=F32)


def tn(a, b):
    return lax.dot_general(a, b, (((0,), (0,)), ((), ())), preferred_element_type=F32)


def fold(rows):
    return jnp.concatenate([rows[:, : D // 2], rows[:, D // 2 :]], axis=0)


def unfold(rows):
    return jnp.concatenate([rows[:8], rows[8:]], axis=1)


def add_all(acc, ref, n):
    for i in range(1, n):
        acc = acc + ref[i].astype(F32)
    return acc


def lanes(shape, columns):
    at = lax.broadcasted_iota(jnp.int32, shape, 1)
    tile = jnp.zeros(shape, F32)
    for i, column in enumerate(columns):
        tile = jnp.where(at == i, column, tile)
    return tile


def split2(value):
    high = value.astype(BF).astype(F32)
    return high, value - high


class Copies:
    def __init__(self, open_copies, make, order, sent, received=None):
        self.make, self.order, self.sent, self.received = make, order, sent, received
        self.to_send = self.to_receive = False
        open_copies.append(self)

    def start(self, d):
        self.to_send = self.to_receive = True
        self.make(d).start()

    def start_all(self):
        for d in self.order:
            self.start(d)

    def wait_recv(self):
        self.to_receive = False
        ref, sem = self.received
        pltpu.make_async_copy(ref, ref, sem).wait()

    def wait_one(self, d):
        self.to_receive = False
        self.make(d).wait_recv()

    def drain(self):
        if self.to_receive:
            if self.received is None:
                for d in self.order:
                    self.wait_one(d)
            else:
                self.wait_recv()
        if self.to_send:
            ref, sem = self.sent
            pltpu.make_async_copy(ref, ref, sem).wait()


class Local:
    def __init__(self, open_copies, *copy):
        self.copy = pltpu.make_async_copy(*copy)
        self.waited = True
        open_copies.append(self)

    def start(self):
        self.waited = False
        self.copy.start()

    def wait(self):
        self.waited = True
        self.copy.wait()

    def drain(self):
        if not self.waited:
            self.wait()


def kernel(
    x_hbm, keys_hbm, wi_hbm, wo_hbm, g_hbm,
    tgs, kout, wigs, wogs,
    x, keys, wi, wo, g,
    keysT, LT, comb, combH, disp, xT,
    gs_send, gs_recv, gsum, gpk, garr,
    us_send, us_recv, usum, ustat, upk, uarr,
    wiT, woT, rown, zg, zu, gall, rall, pre, act, pg, outp,
    cpk, crecv, bpk, brecv,
    so, si, sof, sif, cpart, lgH, lgN, dispH,
    ks_send, ks_recv, ksum, kpk, karr, kz, kzarr,
    ld, send, recv, do_r, db_r,
):
    dp = lax.axis_index("dp")
    ctx = lax.axis_index("ctx")
    core = lax.rem(ctx, 2)
    chip = lax.div(ctx, 2)
    cy, cx = lax.div(chip, SIDE), lax.rem(chip, SIDE)
    other = 1 - core
    sib = {"ctx": chip * 2 + other}

    def ahead(d):
        return lax.rem(cy + d // SIDE, SIDE) * SIDE + lax.rem(cx + d % SIDE, SIDE)

    def behind(d):
        return (
            lax.rem(cy + SIDE - d // SIDE, SIDE) * SIDE
            + lax.rem(cx + SIDE - d % SIDE, SIDE)
        )

    def zahead(e):
        return lax.rem(dp + e, NZ)

    def zbehind(e):
        return lax.rem(dp + NZ - e, NZ)

    open_copies = []

    def remote(src, dst, send, recv, device):
        return pltpu.make_async_remote_copy(
            src_ref=src, dst_ref=dst, send_sem=send, recv_sem=recv,
            device_id=device, device_id_type=MESH,
        )

    load_keys = Local(open_copies, keys_hbm, keys, ld.at[0])
    parts = (slice(0, 256), slice(256, 512), slice(512, T))
    load_x = [Local(open_copies, x_hbm.at[at], x.at[at], ld.at[5 + i]) for i, at in enumerate(parts)]
    load_g = Local(open_copies, g_hbm, g, ld.at[2])
    load_wo = Local(open_copies, wo_hbm, wo, ld.at[3])
    load_wi = Local(open_copies, wi_hbm, wi, ld.at[4])
    for copy in (load_keys, *load_x):
        copy.start()

    barrier = pltpu.get_barrier_semaphore()
    pl.semaphore_signal(barrier, inc=1, device_id=sib, device_id_type=MESH)

    for d in PLANE:
        pl.semaphore_signal(
            barrier, inc=1, device_id={"ctx": ahead(d) * 2 + core}, device_id_type=MESH
        )
    for e in LINE:
        pl.semaphore_signal(barrier, inc=1, device_id={"dp": zahead(e)}, device_id_type=MESH)

    load_keys.wait()
    load_g.start()
    for b in range(D // 128):
        block = keys[b * 128 : (b + 1) * 128, :].astype(F32).T
        keysT[:, b * 128 : (b + 1) * 128] = jnp.concatenate(
            [block[(2 * j + k) * 8 : (2 * j + k) * 8 + 8] for k in range(2) for j in range(NC)], axis=0
        ).astype(BF)
    for copy, part in zip(load_x, parts):
        copy.wait()
        LT[:, part] = nt(keysT[...], x[part, :])
    mine = pl.ds(pl.multiple_of(core * 128, 128), 128)
    theirs = pl.ds(pl.multiple_of(other * 128, 128), 128)
    half = D // 2

    logit = LT[...]
    top = jnp.max(logit, axis=1, keepdims=True).astype(BF).astype(F32)
    e = jnp.exp(logit - top)
    total = jnp.sum(e, axis=1, keepdims=True)
    disp[...] = e.astype(BF)
    high, low = split2(total)
    ustat[...] = lanes((S, 128), (top, high, low))
    us_send[:, :D] = nn(disp[theirs, :], x[...]).astype(BF)
    us_send[:, D:] = ustat[theirs, :].astype(BF)
    pl.semaphore_wait(barrier, NC + NZ - 1)
    sib_u = Copies(
        open_copies, lambda d: remote(us_send, us_recv, send.at[1], recv.at[1], sib), [0],
        (us_send, send.at[1]), (us_recv, recv.at[1]),
    )
    sib_u.start_all()

    for t in range(T // 128):
        at = slice(t * 128, (t + 1) * 128)
        logit = LT[:, at]
        e = jnp.exp(logit - jnp.max(logit, axis=0, keepdims=True))
        e = e / jnp.sum(e, axis=0, keepdims=True)
        comb[:, at] = e
        combH[:, at] = e.astype(BF)
    load_g.wait()
    gs_send[...] = nn(combH[theirs, :], g[...]).astype(BF)
    sib_g = Copies(
        open_copies, lambda d: remote(gs_send, gs_recv, send.at[0], recv.at[0], sib), [0],
        (gs_send, send.at[0]), (gs_recv, recv.at[0]),
    )
    sib_g.start_all()
    usum[...] = nn(disp[mine, :], x[...])

    own = ustat[mine, :]
    sib_u.wait_recv()
    got = us_recv[:, D:].astype(F32)
    top_a, top_b = own[:, 0:1], got[:, 0:1]
    top = jnp.maximum(top_a, top_b)
    wa, wb = jnp.exp(top_a - top), jnp.exp(top_b - top)
    total = (own[:, 1:2] + own[:, 2:3]) * wa + (got[:, 1:2] + got[:, 2:3]) * wb
    usum[...] = usum[...] * wa + us_recv[:, :D].astype(F32) * wb
    high, low = split2(total)
    ustat[0:128, :] = lanes((128, 128), (top, high, low))
    for j in range(NC):
        tile = ustat[j * 8 : j * 8 + 8, :]
        upk[j] = jnp.concatenate(
            [fold(usum[j * 8 : j * 8 + 8, :]), jnp.concatenate([tile, tile], axis=0)], axis=1
        ).astype(BF)

    def au_copy(d):
        j = ahead(d)
        return remote(upk.at[j], uarr.at[d], send.at[4], recv.at[4], {"ctx": j * 2 + core})

    au = Copies(open_copies, au_copy, PLANE, (upk.at[0 : NC - 1], send.at[4]), (uarr.at[1:NC], recv.at[4]))
    au.start_all()
    uarr[0] = upk[chip]

    gsum[...] = nn(combH[mine, :], g[...])
    sib_g.wait_recv()
    gsum[...] += gs_recv[...].astype(F32)

    def ag_copy(d):
        j = ahead(d)
        return remote(gpk.at[j], garr.at[d], send.at[3], recv.at[3], {"ctx": j * 2 + core})

    ag = Copies(open_copies, ag_copy, PLANE, (gpk.at[0 : NC - 1], send.at[3]), (garr.at[1:NC], recv.at[3]))
    for j in range(NC):
        gpk[j] = fold(gsum[j * 8 : j * 8 + 8, :]).astype(BF)
    ag.start_all()
    load_wi.start()
    load_wo.start()

    for b in range(D // 128):
        block = x[:, b * 128 : (b + 1) * 128].T
        xT[0, b * 64 : (b + 1) * 64, :] = jnp.concatenate([block[0:32], block[64:96]], axis=0)
        xT[1, b * 64 : (b + 1) * 64, :] = jnp.concatenate([block[32:64], block[96:128]], axis=0)

    load_wi.wait()
    load_wo.wait()
    for e in range(2):
        for b in range(D // 128):
            at = slice(b * 128, (b + 1) * 128)
            wiT[e, :, at] = wi[e, at, :].T
        for b in range(HL // 128):
            at = slice(b * 128, (b + 1) * 128)
            woT[e, :, at] = wo[e, at, :].T

    au.wait_recv()
    stats = uarr[:, :, half : half + 128].astype(F32)
    top = jnp.max(stats[:, :, 0:1], axis=0)
    w = jnp.exp(stats[:, :, 0:1] - top)
    total = jnp.sum(w * (stats[:, :, 1:2] + stats[:, :, 2:3]), axis=0)
    acc = jnp.zeros((16, half), F32)
    for d in range(NC):
        acc = acc + w[d] * uarr[d, :, :half].astype(F32)
    acc = acc / total
    rown[...] = acc
    zu[dp] = acc.astype(BF)

    def bu_copy(e):
        return remote(zu.at[dp], zu.at[dp], send.at[6], recv.at[6], {"dp": zahead(e)})

    bu = Copies(open_copies, bu_copy, LINE, (zu.at[0 : NZ - 1], send.at[6]), (zu.at[0 : NZ - 1], recv.at[6]))
    bu.start_all()
    z_high, z_low = split2(total)
    so[core, chip, :, half:] = lanes((16, 128), (top, z_high, z_low)).astype(BF)

    acc = fold(gsum[pl.ds(pl.multiple_of(chip * 8, 8), 8), :])
    ag.wait_recv()
    zg[dp] = add_all(acc, garr, NC).astype(BF)

    def bg_copy(e):
        return remote(zg.at[dp], zg.at[dp], send.at[5], recv.at[5], {"dp": zahead(e)})

    bg = Copies(open_copies, bg_copy, LINE, (zg.at[0 : NZ - 1], send.at[5]), (zg.at[0 : NZ - 1], recv.at[5]))
    bg.start_all()

    first = lax.rem(lax.broadcasted_iota(jnp.int32, (64, HL), 0), 8) < 4
    bu.wait_recv()
    rall[...] = jnp.concatenate([unfold(zu[c].astype(F32)) for c in range(NZ)], axis=0).astype(BF)
    pre_act = jnp.where(first, nn(rall[...], wi[0]), nn(rall[...], wi[1]))
    a = gelu_value(pre_act)
    act[0] = jnp.where(first, a, 0.0).astype(BF)
    act[1] = jnp.where(first, 0.0, a).astype(BF)
    pre[...] = gelu_slope(pre_act)
    outp[...] = nn(act[0], wo[0]) + nn(act[1], wo[1])

    def co_copy(e):
        j = zahead(e)
        return remote(cpk.at[j], crecv.at[e], send.at[7], recv.at[7], {"dp": j})

    co = Copies(open_copies, co_copy, LINE, (cpk.at[0 : NZ - 1], send.at[7]), (crecv.at[1:NZ], recv.at[7]))
    for j in range(NZ):
        cpk[j] = fold(outp[j * 8 : j * 8 + 8, :]).astype(BF)
    co.start_all()
    o_own = fold(outp[pl.ds(pl.multiple_of(dp * 8, 8), 8), :])

    bg.wait_recv()
    gall[...] = jnp.concatenate([unfold(zg[c].astype(F32)) for c in range(NZ)], axis=0).astype(BF)
    p = jnp.where(first, nn(gall[...], woT[0]), nn(gall[...], woT[1])) * pre[...]
    pg[0] = jnp.where(first, p, 0.0).astype(BF)
    pg[1] = jnp.where(first, 0.0, p).astype(BF)
    outp[...] = nn(pg[0], wiT[0]) + nn(pg[1], wiT[1])

    def cb_copy(e):
        j = zahead(e)
        return remote(bpk.at[j], brecv.at[e], send.at[8], recv.at[8], {"dp": j})

    cb = Copies(open_copies, cb_copy, LINE, (bpk.at[0 : NZ - 1], send.at[8]), (brecv.at[1:NZ], recv.at[8]))
    for j in range(NZ):
        bpk[j] = fold(outp[j * 8 : j * 8 + 8, :]).astype(BF)
    cb.start_all()
    b_own = fold(outp[pl.ds(pl.multiple_of(dp * 8, 8), 8), :])

    co.wait_recv()
    so[core, chip, :, :half] = add_all(o_own, crecv, NZ).astype(BF)

    def do_copy(d):
        return remote(
            so.at[core, chip], so.at[core, chip], send.at[9], do_r.at[d], {"ctx": ahead(d) * 2 + core}
        )

    def fo_copy(d):
        j = behind(d)
        return remote(so.at[core, j], so.at[core, j], send.at[11], recv.at[11], sib)

    do = Copies(open_copies, do_copy, PLANE, (so.at[0, 0 : NC - 1], send.at[9]))
    fo = Copies(open_copies, fo_copy, [], (so.at[0], send.at[11]), (so.at[0], recv.at[11]))
    do.start_all()
    fo.start(0)

    for e in range(2):
        for c in range(HL // 128):
            at = slice(c * 128, (c + 1) * 128)
            wogs[e, at, :] = tn(act[e, :, at], gall[...]).astype(BF)
        for c in range(D // 128):
            at = slice(c * 128, (c + 1) * 128)
            wigs[e, at, :] = tn(rall[:, at], pg[e]).astype(BF)

    cb.wait_recv()
    back = add_all(b_own, brecv, NZ).astype(BF)
    si[core, chip, :, :half] = back
    inner = jnp.sum(rown[...] * back.astype(F32), axis=1, keepdims=True)
    inner = inner[:8] + inner[8:]
    inner = jnp.concatenate([inner, inner], axis=0)
    i_high, i_low = split2(inner)
    si[core, chip, :, half:] = lanes((16, 128), (i_high, i_low)).astype(BF)

    def db_copy(d):
        return remote(
            si.at[core, chip], si.at[core, chip], send.at[10], db_r.at[d], {"ctx": ahead(d) * 2 + core}
        )

    def fb_copy(d):
        j = behind(d)
        return remote(si.at[core, j], si.at[core, j], send.at[12], recv.at[12], sib)

    db = Copies(open_copies, db_copy, PLANE, (si.at[0, 0 : NC - 1], send.at[10]))
    fb = Copies(open_copies, fb_copy, [], (si.at[0], send.at[12]), (si.at[0], recv.at[12]))
    db.start_all()
    fb.start(0)

    for d in reversed(PLANE):
        do.wait_one(d)
        fo.start(d)

    def gather(ref, rows, k):
        for q in range(NC // 2):
            rows[pl.ds(pl.multiple_of(k * 128 + q * 16, 16), 16), :] = jnp.concatenate(
                [unfold(ref[k, 2 * q + i, :, :half].astype(F32)) for i in range(2)], axis=0
            ).astype(BF)

    def stat_of(ref):
        return jnp.concatenate(
            [ref[k, j, 0:8, half : half + 128].astype(F32) for k in range(2) for j in range(NC)], axis=0
        )

    gather(so, sof, core)
    cpart[mine, :] = nt(sof[mine, :], g[...])
    fo.wait_recv()
    gather(so, sof, other)
    cpart[theirs, :] = nt(sof[theirs, :], g[...])
    stat = stat_of(so)
    top = stat[:, 0:1]
    over = 1.0 / (stat[:, 1:2] + stat[:, 2:3])
    for t in range(T // 128):
        at = slice(t * 128, (t + 1) * 128)
        prob, back = comb[:, at], cpart[:, at]
        cpart[:, at] = prob * (back - jnp.sum(prob * back, axis=0, keepdims=True))
        prob = jnp.exp(LT[:, at] - top) * over
        LT[:, at] = prob
        dispH[:, at] = prob.astype(BF)

    for d in reversed(PLANE):
        db.wait_one(d)
        fb.start(d)
    gather(si, sif, core)
    comb[mine, :] = nt(sif[mine, :], x[...])
    fb.wait_recv()
    gather(si, sif, other)
    comb[theirs, :] = nt(sif[theirs, :], x[...])
    stat = stat_of(si)
    inner = stat[:, 0:1] + stat[:, 1:2]
    for t in range(T // 128):
        at = slice(t * 128, (t + 1) * 128)
        lg = LT[:, at] * (comb[:, at] - inner) + cpart[:, at]
        lgH[:, at] = lg.astype(BF)
        lgN[:, at] = jnp.concatenate(
            [lg[k * 128 + j * 8 : k * 128 + j * 8 + 8] for j in range(NC) for k in range(2)], axis=0
        ).astype(BF)

    ks_send[...] = nt(xT[other], lgN[...]).astype(BF)
    sib_k = Copies(
        open_copies, lambda d: remote(ks_send, ks_recv, send.at[2], recv.at[2], sib), [0],
        (ks_send, send.at[2]), (ks_recv, recv.at[2]),
    )
    sib_k.start_all()
    ksum[...] = nt(xT[core], lgN[...])
    sib_k.wait_recv()
    ksum[...] += ks_recv[...].astype(F32)

    def fk_copy(d):
        j = ahead(d)
        return remote(kpk.at[j], karr.at[d], send.at[13], recv.at[13], {"ctx": j * 2 + core})

    fk = Copies(open_copies, fk_copy, PLANE, (kpk.at[0 : NC - 1], send.at[13]), (karr.at[1:NC], recv.at[13]))

    for j in range(NC):
        kpk[j] = ksum[j * 32 : j * 32 + 32, :].astype(BF)
    fk.start_all()

    for t in range(T // 128):
        at = slice(t * 128, (t + 1) * 128)
        tgs[at, :] = (tn(lgH[:, at], keysT[...]) + tn(dispH[:, at], sif[...])).astype(BF)

    fk.wait_recv()
    acc = add_all(ksum[pl.ds(pl.multiple_of(chip * 32, 32), 32), :], karr, NC)
    kz[...] = acc.astype(BF)

    def fz_copy(e):
        return remote(kz, kzarr.at[e], send.at[14], recv.at[14], {"dp": zahead(e)})

    fz = Copies(open_copies, fz_copy, LINE, (kzarr.at[0 : NZ - 1], send.at[14]), (kzarr.at[1:NZ], recv.at[14]))


    fz.start_all()

    fz.wait_recv()
    kout[...] = add_all(acc, kzarr, NZ)

    for copies in open_copies:
        copies.drain()


def store_kernel(tgs, kout, wigs, wogs, tg_hbm, kg_hbm, wig_hbm, wog_hbm, st):
    pairs = ((wigs, wig_hbm), (wogs, wog_hbm), (tgs, tg_hbm), (kout, kg_hbm))
    copies = [pltpu.make_async_copy(src, dst, st.at[i]) for i, (src, dst) in enumerate(pairs)]
    for copy in copies:
        copy.start()
    for copy in copies:
        copy.wait()


def per_device(tokens, slot_keys, w_in, w_out, out_grad):
    hbm = pl.BlockSpec(memory_space=pltpu.HBM)
    vmem = pltpu.VMEM
    half = D // 2
    held = pl.pallas_call(
        kernel,
        out_shape=(
            pltpu.VMEM((T, D), BF),
            pltpu.VMEM((32, S), F32),
            pltpu.VMEM((2, D, HL), BF),
            pltpu.VMEM((2, HL, D), BF),
        ),
        in_specs=[hbm] * 5,
        out_specs=(pl.BlockSpec(memory_space=vmem),) * 4,
        scratch_shapes=[
            vmem((T, D), BF), vmem((D, S), BF), vmem((2, D, HL), BF), vmem((2, HL, D), BF), vmem((T, D), BF),
            vmem((S, D), BF), vmem((S, T), F32), vmem((S, T), F32), vmem((S, T), BF), vmem((S, T), BF),
            vmem((2, D // 2, T), BF),
            vmem((128, D), BF), vmem((128, D), BF), vmem((128, D), F32),
            vmem((NC, 16, half), BF), vmem((NC, 16, half), BF),
            vmem((128, D + 128), BF), vmem((128, D + 128), BF), vmem((128, D), F32), vmem((S, 128), F32),
            vmem((NC, 16, half + 128), BF), vmem((NC, 16, half + 128), BF),
            vmem((2, HL, D), BF), vmem((2, D, HL), BF),
            vmem((16, half), F32), vmem((NZ, 16, half), BF), vmem((NZ, 16, half), BF),
            vmem((64, D), BF), vmem((64, D), BF), vmem((64, HL), F32),
            vmem((2, 64, HL), BF), vmem((2, 64, HL), BF), vmem((64, D), F32),
            vmem((NZ, 16, half), BF), vmem((NZ, 16, half), BF),
            vmem((NZ, 16, half), BF), vmem((NZ, 16, half), BF),
            vmem((2, NC, 16, half + 128), BF), vmem((2, NC, 16, half + 128), BF), vmem((S, D), BF), vmem((S, D), BF),
            vmem((S, T), F32), vmem((S, T), BF), vmem((S, T), BF), vmem((S, T), BF),
            vmem((D // 2, S), BF), vmem((D // 2, S), BF), vmem((D // 2, S), F32),
            vmem((NC, 32, S), BF), vmem((NC, 32, S), BF), vmem((32, S), BF), vmem((NZ, 32, S), BF),
            pltpu.SemaphoreType.DMA((8,)), pltpu.SemaphoreType.DMA((15,)), pltpu.SemaphoreType.DMA((15,)),
            pltpu.SemaphoreType.DMA((NC,)), pltpu.SemaphoreType.DMA((NC,)),
        ],
        compiler_params=pltpu.CompilerParams(
            collective_id=0, has_side_effects=True, vmem_limit_bytes=36 * 2**20
        ),
        cost_estimate=pl.CostEstimate(flops=4 * 10**9, bytes_accessed=13 * 10**6, transcendentals=10**6),
    )(*(pltpu.with_memory_space_constraint(a, pltpu.HBM) for a in (tokens[0], slot_keys, w_in, w_out, out_grad[0])))
    tg, kg, wig, wog = pl.pallas_call(
        store_kernel,
        out_shape=(
            pltpu.HBM((T, D), BF),
            pltpu.HBM((32, S), F32),
            pltpu.HBM((2, D, HL), BF),
            pltpu.HBM((2, HL, D), BF),
        ),
        in_specs=[pl.BlockSpec(memory_space=vmem)] * 4,
        out_specs=(hbm,) * 4,
        scratch_shapes=[pltpu.SemaphoreType.DMA((4,))],
        compiler_params=pltpu.CompilerParams(vmem_limit_bytes=2**20),
    )(*held)
    return tg[None], kg, wig, wog


def solution(mesh):
    return jax.shard_map(
        per_device,
        mesh=mesh,
        in_specs=(
            P("dp", "ctx", None),
            P(),
            P("ctx", None, "dp"),
            P("ctx", "dp", None),
            P("dp", "ctx", None),
        ),
        out_specs=(
            P("dp", "ctx", None),
            P("ctx", None),
            P("ctx", None, "dp"),
            P("ctx", "dp", None),
        ),
        check_vma=False,
    )
```

```python
import jax
import jax.numpy as jnp
from jax import lax
from jax.experimental import pallas as pl
from jax.experimental.pallas import tpu as pltpu
from jax.sharding import PartitionSpec as P

MESH = pl.DeviceIdType.MESH
BF = jnp.bfloat16
F32 = jnp.float32

T = 640
D = 1024
S = 256
HL = 512
NZ = 8
SIDE = 4
NC = SIDE * SIDE

PLANE = sorted(range(1, NC), key=lambda d: -sum(min(i, SIDE - i) for i in divmod(d, SIDE)))
LINE = sorted(range(1, NZ), key=lambda e: -min(e, NZ - e))

GELU_A = 0.7978845608028654
GELU_B = 0.044715


def gelu_value(value):
    return 0.5 * value * (1.0 + jnp.tanh(GELU_A * (value + GELU_B * value * value * value)))


def gelu_slope(value):
    inner = jnp.tanh(GELU_A * (value + GELU_B * value * value * value))
    return 0.5 * (1.0 + inner) + 0.5 * value * (1.0 - inner * inner) * GELU_A * (
        1.0 + 3.0 * GELU_B * value * value
    )


def nn(a, b):
    return lax.dot_general(a, b, (((1,), (0,)), ((), ())), preferred_element_type=F32)


def nt(a, b):
    return lax.dot_general(a, b, (((1,), (1,)), ((), ())), preferred_element_type=F32)


def tn(a, b):
    return lax.dot_general(a, b, (((0,), (0,)), ((), ())), preferred_element_type=F32)


def fold(rows):
    return jnp.concatenate([rows[:, : D // 2], rows[:, D // 2 :]], axis=0)


def unfold(rows):
    return jnp.concatenate([rows[:8], rows[8:]], axis=1)


def add_all(acc, ref, n):
    for i in range(1, n):
        acc = acc + ref[i].astype(F32)
    return acc


def lanes(shape, columns):
    at = lax.broadcasted_iota(jnp.int32, shape, 1)
    tile = jnp.zeros(shape, F32)
    for i, column in enumerate(columns):
        tile = jnp.where(at == i, column, tile)
    return tile


def split2(value):
    high = value.astype(BF).astype(F32)
    return high, value - high


class Copies:
    def __init__(self, open_copies, make, order, sent, received=None):
        self.make, self.order, self.sent, self.received = make, order, sent, received
        self.to_send = self.to_receive = False
        open_copies.append(self)

    def start(self, d):
        self.to_send = self.to_receive = True
        self.make(d).start()

    def start_all(self):
        for d in self.order:
            self.start(d)

    def wait_recv(self):
        self.to_receive = False
        ref, sem = self.received
        pltpu.make_async_copy(ref, ref, sem).wait()

    def wait_one(self, d):
        self.to_receive = False
        self.make(d).wait_recv()

    def drain(self):
        if self.to_receive:
            if self.received is None:
                for d in self.order:
                    self.wait_one(d)
            else:
                self.wait_recv()
        if self.to_send:
            ref, sem = self.sent
            pltpu.make_async_copy(ref, ref, sem).wait()


class Local:
    def __init__(self, open_copies, *copy):
        self.copy = pltpu.make_async_copy(*copy)
        self.waited = True
        open_copies.append(self)

    def start(self):
        self.waited = False
        self.copy.start()

    def wait(self):
        self.waited = True
        self.copy.wait()

    def drain(self):
        if not self.waited:
            self.wait()


def kernel(
    x_hbm, keys_hbm, wi_hbm, wo_hbm, g_hbm,
    tgs, kout, wigs, wogs,
    x, keys, wi, wo, g,
    keysT, LT, comb, combH, disp, xT,
    gs_send, gs_recv, gsum, gpk, garr,
    us_send, us_recv, usum, ustat, upk, uarr, ust, ustr, utt,
    wiT, woT, rown, zg, zu, gall, rall, pre, act, pg, outp,
    cpk, crecv, bpk, brecv,
    so, si, sm, sof, sif, cpart, lgH, lgN, dispH,
    ks_send, ks_recv, ksum, kpk, karr, kz, kzarr,
    ld, send, recv, do_r, db_r, dm_r,
):
    dp = lax.axis_index("dp")
    ctx = lax.axis_index("ctx")
    core = lax.rem(ctx, 2)
    chip = lax.div(ctx, 2)
    cy, cx = lax.div(chip, SIDE), lax.rem(chip, SIDE)
    other = 1 - core
    sib = {"ctx": chip * 2 + other}

    def ahead(d):
        return lax.rem(cy + d // SIDE, SIDE) * SIDE + lax.rem(cx + d % SIDE, SIDE)

    def behind(d):
        return (
            lax.rem(cy + SIDE - d // SIDE, SIDE) * SIDE
            + lax.rem(cx + SIDE - d % SIDE, SIDE)
        )

    def zahead(e):
        return lax.rem(dp + e, NZ)

    def zbehind(e):
        return lax.rem(dp + NZ - e, NZ)

    open_copies = []

    def remote(src, dst, send, recv, device):
        return pltpu.make_async_remote_copy(
            src_ref=src, dst_ref=dst, send_sem=send, recv_sem=recv,
            device_id=device, device_id_type=MESH,
        )

    load_keys = Local(open_copies, keys_hbm, keys, ld.at[0])
    load_x = Local(open_copies, x_hbm, x, ld.at[1])
    load_g = Local(open_copies, g_hbm, g, ld.at[2])
    load_wo = Local(open_copies, wo_hbm, wo, ld.at[3])
    load_wi = Local(open_copies, wi_hbm, wi, ld.at[4])
    load_keys.start()
    load_x.start()

    barrier = pltpu.get_barrier_semaphore()
    pl.semaphore_signal(barrier, inc=1, device_id=sib, device_id_type=MESH)

    for d in PLANE:
        pl.semaphore_signal(
            barrier, inc=1, device_id={"ctx": ahead(d) * 2 + core}, device_id_type=MESH
        )
    for e in LINE:
        pl.semaphore_signal(barrier, inc=1, device_id={"dp": zahead(e)}, device_id_type=MESH)

    load_keys.wait()
    load_g.start()
    for b in range(D // 128):
        block = keys[b * 128 : (b + 1) * 128, :].astype(F32).T
        keysT[:, b * 128 : (b + 1) * 128] = jnp.concatenate(
            [block[(2 * j + k) * 8 : (2 * j + k) * 8 + 8] for k in range(2) for j in range(NC)], axis=0
        ).astype(BF)
    load_x.wait()
    LT[...] = nt(keysT[...], x[...])
    mine = pl.ds(pl.multiple_of(core * 128, 128), 128)
    theirs = pl.ds(pl.multiple_of(other * 128, 128), 128)
    half = D // 2

    logit = LT[...]
    top = jnp.max(logit, axis=1, keepdims=True).astype(BF).astype(F32)
    e = jnp.exp(logit - top)
    total = jnp.sum(e, axis=1, keepdims=True)
    disp[...] = e.astype(BF)
    high, low = split2(total)
    ustat[...] = lanes((S, 128), (top, high, low))
    us_send[:, :D] = nn(disp[theirs, :], x[...]).astype(BF)
    us_send[:, D:] = ustat[theirs, :].astype(BF)
    pl.semaphore_wait(barrier, NC + NZ - 1)
    sib_u = Copies(
        open_copies, lambda d: remote(us_send, us_recv, send.at[1], recv.at[1], sib), [0],
        (us_send, send.at[1]), (us_recv, recv.at[1]),
    )
    sib_u.start_all()

    for t in range(T // 128):
        at = slice(t * 128, (t + 1) * 128)
        logit = LT[:, at]
        e = jnp.exp(logit - jnp.max(logit, axis=0, keepdims=True))
        e = e / jnp.sum(e, axis=0, keepdims=True)
        comb[:, at] = e
        combH[:, at] = e.astype(BF)
    load_g.wait()
    gs_send[...] = nn(combH[theirs, :], g[...]).astype(BF)
    sib_g = Copies(
        open_copies, lambda d: remote(gs_send, gs_recv, send.at[0], recv.at[0], sib), [0],
        (gs_send, send.at[0]), (gs_recv, recv.at[0]),
    )
    sib_g.start_all()
    usum[...] = nn(disp[mine, :], x[...])

    own = ustat[mine, :]
    sib_u.wait_recv()
    got = us_recv[:, D:].astype(F32)
    top_a, top_b = own[:, 0:1], got[:, 0:1]
    top = jnp.maximum(top_a, top_b)
    wa, wb = jnp.exp(top_a - top), jnp.exp(top_b - top)
    total = (own[:, 1:2] + own[:, 2:3]) * wa + (got[:, 1:2] + got[:, 2:3]) * wb
    usum[...] = usum[...] * wa + us_recv[:, :D].astype(F32) * wb
    ust[...] = lanes((128, 128), (top, total)).T[0:2, :]
    for j in range(NC):
        upk[j] = fold(usum[j * 8 : j * 8 + 8, :]).astype(BF)

    def aw_copy(d):
        return remote(ust, ustr.at[d], send.at[17], recv.at[16], {"ctx": ahead(d) * 2 + core})

    aw = Copies(open_copies, aw_copy, PLANE, (ustr.at[1:NC], send.at[17]), (ustr.at[1:NC], recv.at[16]))
    aw.start_all()

    def au_copy(d):
        j = ahead(d)
        return remote(upk.at[j], uarr.at[d], send.at[4], recv.at[4], {"ctx": j * 2 + core})

    au = Copies(open_copies, au_copy, PLANE, (upk.at[0 : NC - 1], send.at[4]), (uarr.at[1:NC], recv.at[4]))
    au.start_all()
    uarr[0] = upk[chip]
    ustr[0] = ust[...]

    gsum[...] = nn(combH[mine, :], g[...])
    sib_g.wait_recv()
    gsum[...] += gs_recv[...].astype(F32)

    def ag_copy(d):
        j = ahead(d)
        return remote(gpk.at[j], garr.at[d], send.at[3], recv.at[3], {"ctx": j * 2 + core})

    ag = Copies(open_copies, ag_copy, PLANE, (gpk.at[0 : NC - 1], send.at[3]), (garr.at[1:NC], recv.at[3]))
    for j in range(NC):
        gpk[j] = fold(gsum[j * 8 : j * 8 + 8, :]).astype(BF)
    ag.start_all()
    load_wi.start()
    load_wo.start()

    for b in range(D // 128):
        block = x[:, b * 128 : (b + 1) * 128].T
        xT[0, b * 64 : (b + 1) * 64, :] = jnp.concatenate([block[0:32], block[64:96]], axis=0)
        xT[1, b * 64 : (b + 1) * 64, :] = jnp.concatenate([block[32:64], block[96:128]], axis=0)

    load_wi.wait()
    load_wo.wait()
    for e in range(2):
        for b in range(D // 128):
            at = slice(b * 128, (b + 1) * 128)
            wiT[e, :, at] = wi[e, at, :].T
        for b in range(HL // 128):
            at = slice(b * 128, (b + 1) * 128)
            woT[e, :, at] = wo[e, at, :].T

    au.wait_recv()
    aw.wait_recv()
    utt[...] = jnp.concatenate(
        [ustr[:, 0, :], ustr[:, 1, :], jnp.zeros((128 - 2 * NC, 128), F32)], axis=0
    ).T
    stats = utt[pl.ds(pl.multiple_of(chip * 8, 8), 8), :]
    stats = jnp.concatenate([stats, stats], axis=0)
    top = jnp.max(stats[:, :NC], axis=1, keepdims=True)
    w = jnp.exp(stats[:, :NC] - top)
    total = jnp.sum(w * stats[:, NC : 2 * NC], axis=1, keepdims=True)
    acc = jnp.zeros((16, half), F32)
    for d in range(NC):
        acc = acc + w[:, d : d + 1] * uarr[d].astype(F32)
    acc = acc / total
    rown[...] = acc
    zu[dp] = acc.astype(BF)

    def bu_copy(e):
        return remote(zu.at[dp], zu.at[dp], send.at[6], recv.at[6], {"dp": zahead(e)})

    bu = Copies(open_copies, bu_copy, LINE, (zu.at[0 : NZ - 1], send.at[6]), (zu.at[0 : NZ - 1], recv.at[6]))
    bu.start_all()
    z_high, z_low = split2(total)
    sm[core, chip] = lanes((16, 128), (top, z_high, z_low)).astype(BF)

    acc = fold(gsum[pl.ds(pl.multiple_of(chip * 8, 8), 8), :])
    ag.wait_recv()
    zg[dp] = add_all(acc, garr, NC).astype(BF)

    def bg_copy(e):
        return remote(zg.at[dp], zg.at[dp], send.at[5], recv.at[5], {"dp": zahead(e)})

    bg = Copies(open_copies, bg_copy, LINE, (zg.at[0 : NZ - 1], send.at[5]), (zg.at[0 : NZ - 1], recv.at[5]))
    bg.start_all()

    def dm_copy(d):
        return remote(
            sm.at[core, chip], sm.at[core, chip], send.at[15], dm_r.at[d], {"ctx": ahead(d) * 2 + core}
        )

    def fm_copy(d):
        j = behind(d)
        return remote(sm.at[core, j], sm.at[core, j], send.at[16], recv.at[15], sib)

    dm = Copies(open_copies, dm_copy, PLANE, (sm.at[0, 0 : NC - 1], send.at[15]))
    fm = Copies(open_copies, fm_copy, [], (sm.at[0], send.at[16]), (sm.at[0], recv.at[15]))
    dm.start_all()
    fm.start(0)

    first = lax.rem(lax.broadcasted_iota(jnp.int32, (64, HL), 0), 8) < 4
    bu.wait_recv()
    rall[...] = jnp.concatenate([unfold(zu[c].astype(F32)) for c in range(NZ)], axis=0).astype(BF)
    pre_act = jnp.where(first, nn(rall[...], wi[0]), nn(rall[...], wi[1]))
    a = gelu_value(pre_act)
    act[0] = jnp.where(first, a, 0.0).astype(BF)
    act[1] = jnp.where(first, 0.0, a).astype(BF)
    pre[...] = gelu_slope(pre_act)
    outp[...] = nn(act[0], wo[0]) + nn(act[1], wo[1])

    def co_copy(e):
        j = zahead(e)
        return remote(cpk.at[j], crecv.at[e], send.at[7], recv.at[7], {"dp": j})

    co = Copies(open_copies, co_copy, LINE, (cpk.at[0 : NZ - 1], send.at[7]), (crecv.at[1:NZ], recv.at[7]))
    for j in range(NZ):
        cpk[j] = fold(outp[j * 8 : j * 8 + 8, :]).astype(BF)
    co.start_all()
    o_own = fold(outp[pl.ds(pl.multiple_of(dp * 8, 8), 8), :])

    bg.wait_recv()
    gall[...] = jnp.concatenate([unfold(zg[c].astype(F32)) for c in range(NZ)], axis=0).astype(BF)
    p = jnp.where(first, nn(gall[...], woT[0]), nn(gall[...], woT[1])) * pre[...]
    pg[0] = jnp.where(first, p, 0.0).astype(BF)
    pg[1] = jnp.where(first, 0.0, p).astype(BF)
    outp[...] = nn(pg[0], wiT[0]) + nn(pg[1], wiT[1])

    def cb_copy(e):
        j = zahead(e)
        return remote(bpk.at[j], brecv.at[e], send.at[8], recv.at[8], {"dp": j})

    cb = Copies(open_copies, cb_copy, LINE, (bpk.at[0 : NZ - 1], send.at[8]), (brecv.at[1:NZ], recv.at[8]))
    for j in range(NZ):
        bpk[j] = fold(outp[j * 8 : j * 8 + 8, :]).astype(BF)
    cb.start_all()
    b_own = fold(outp[pl.ds(pl.multiple_of(dp * 8, 8), 8), :])

    for d in reversed(PLANE):
        dm.wait_one(d)
        fm.start(d)

    co.wait_recv()
    so[core, chip] = add_all(o_own, crecv, NZ).astype(BF)

    def do_copy(d):
        return remote(
            so.at[core, chip], so.at[core, chip], send.at[9], do_r.at[d], {"ctx": ahead(d) * 2 + core}
        )

    def fo_copy(d):
        j = behind(d)
        return remote(so.at[core, j], so.at[core, j], send.at[11], recv.at[11], sib)

    do = Copies(open_copies, do_copy, PLANE, (so.at[0, 0 : NC - 1], send.at[9]))
    fo = Copies(open_copies, fo_copy, [], (so.at[0], send.at[11]), (so.at[0], recv.at[11]))
    do.start_all()
    fo.start(0)

    for e in range(2):
        for c in range(HL // 128):
            at = slice(c * 128, (c + 1) * 128)
            wogs[e, at, :] = tn(act[e, :, at], gall[...]).astype(BF)

    def stat_of(ref, low):
        return jnp.concatenate(
            [ref[k, j, 0:8, low : low + 128].astype(F32) for k in range(2) for j in range(NC)], axis=0
        )

    fm.wait_recv()
    stat = stat_of(sm, 0)
    top = stat[:, 0:1]
    over = 1.0 / (stat[:, 1:2] + stat[:, 2:3])
    for t in range(T // 128):
        at = slice(t * 128, (t + 1) * 128)
        prob = jnp.exp(LT[:, at] - top) * over
        LT[:, at] = prob
        dispH[:, at] = prob.astype(BF)

    cb.wait_recv()
    back = add_all(b_own, brecv, NZ).astype(BF)
    si[core, chip, :, :half] = back
    inner = jnp.sum(rown[...] * back.astype(F32), axis=1, keepdims=True)
    inner = inner[:8] + inner[8:]
    inner = jnp.concatenate([inner, inner], axis=0)
    i_high, i_low = split2(inner)
    si[core, chip, :, half:] = lanes((16, 128), (i_high, i_low)).astype(BF)

    def db_copy(d):
        return remote(
            si.at[core, chip], si.at[core, chip], send.at[10], db_r.at[d], {"ctx": ahead(d) * 2 + core}
        )

    def fb_copy(d):
        j = behind(d)
        return remote(si.at[core, j], si.at[core, j], send.at[12], recv.at[12], sib)

    db = Copies(open_copies, db_copy, PLANE, (si.at[0, 0 : NC - 1], send.at[10]))
    fb = Copies(open_copies, fb_copy, [], (si.at[0], send.at[12]), (si.at[0], recv.at[12]))
    db.start_all()
    fb.start(0)
    for e in range(2):
        for c in range(D // 128):
            at = slice(c * 128, (c + 1) * 128)
            wigs[e, at, :] = tn(rall[:, at], pg[e]).astype(BF)

    def gather(ref, rows, k):
        for q in range(NC // 2):
            rows[pl.ds(pl.multiple_of(k * 128 + q * 16, 16), 16), :] = jnp.concatenate(
                [unfold(ref[k, 2 * q + i, :, :half].astype(F32)) for i in range(2)], axis=0
            ).astype(BF)

    for d in reversed(PLANE):
        do.wait_one(d)
        fo.start(d)
    gather(so, sof, core)
    cpart[mine, :] = nt(sof[mine, :], g[...])
    for d in reversed(PLANE):
        db.wait_one(d)
        fb.start(d)
    fo.wait_recv()
    gather(so, sof, other)
    cpart[theirs, :] = nt(sof[theirs, :], g[...])
    for t in range(T // 128):
        at = slice(t * 128, (t + 1) * 128)
        prob, back = comb[:, at], cpart[:, at]
        cpart[:, at] = prob * (back - jnp.sum(prob * back, axis=0, keepdims=True))
    gather(si, sif, core)
    comb[mine, :] = nt(sif[mine, :], x[...])
    fb.wait_recv()
    gather(si, sif, other)
    comb[theirs, :] = nt(sif[theirs, :], x[...])
    stat = stat_of(si, half)
    inner = stat[:, 0:1] + stat[:, 1:2]
    for t in range(T // 128):
        at = slice(t * 128, (t + 1) * 128)
        lg = LT[:, at] * (comb[:, at] - inner) + cpart[:, at]
        lgH[:, at] = lg.astype(BF)
        lgN[:, at] = jnp.concatenate(
            [lg[k * 128 + j * 8 : k * 128 + j * 8 + 8] for j in range(NC) for k in range(2)], axis=0
        ).astype(BF)

    ks_send[...] = nt(xT[other], lgN[...]).astype(BF)
    sib_k = Copies(
        open_copies, lambda d: remote(ks_send, ks_recv, send.at[2], recv.at[2], sib), [0],
        (ks_send, send.at[2]), (ks_recv, recv.at[2]),
    )
    sib_k.start_all()
    ksum[...] = nt(xT[core], lgN[...])
    sib_k.wait_recv()
    ksum[...] += ks_recv[...].astype(F32)

    def fk_copy(d):
        j = ahead(d)
        return remote(kpk.at[j], karr.at[d], send.at[13], recv.at[13], {"ctx": j * 2 + core})

    fk = Copies(open_copies, fk_copy, PLANE, (kpk.at[0 : NC - 1], send.at[13]), (karr.at[1:NC], recv.at[13]))

    for j in range(NC):
        kpk[j] = ksum[j * 32 : j * 32 + 32, :].astype(BF)
    fk.start_all()

    for t in range(T // 128):
        at = slice(t * 128, (t + 1) * 128)
        tgs[at, :] = (tn(lgH[:, at], keysT[...]) + tn(dispH[:, at], sif[...])).astype(BF)

    fk.wait_recv()
    acc = add_all(ksum[pl.ds(pl.multiple_of(chip * 32, 32), 32), :], karr, NC)
    kz[...] = acc.astype(BF)

    def fz_copy(e):
        return remote(kz, kzarr.at[e], send.at[14], recv.at[14], {"dp": zahead(e)})

    fz = Copies(open_copies, fz_copy, LINE, (kzarr.at[0 : NZ - 1], send.at[14]), (kzarr.at[1:NZ], recv.at[14]))


    fz.start_all()

    fz.wait_recv()
    kout[...] = add_all(acc, kzarr, NZ)

    for copies in open_copies:
        copies.drain()


def store_kernel(tgs, kout, wigs, wogs, tg_hbm, kg_hbm, wig_hbm, wog_hbm, st):
    pairs = ((wigs, wig_hbm), (wogs, wog_hbm), (tgs, tg_hbm), (kout, kg_hbm))
    copies = [pltpu.make_async_copy(src, dst, st.at[i]) for i, (src, dst) in enumerate(pairs)]
    for copy in copies:
        copy.start()
    for copy in copies:
        copy.wait()


def per_device(tokens, slot_keys, w_in, w_out, out_grad):
    hbm = pl.BlockSpec(memory_space=pltpu.HBM)
    vmem = pltpu.VMEM
    half = D // 2
    held = pl.pallas_call(
        kernel,
        out_shape=(
            pltpu.VMEM((T, D), BF),
            pltpu.VMEM((32, S), F32),
            pltpu.VMEM((2, D, HL), BF),
            pltpu.VMEM((2, HL, D), BF),
        ),
        in_specs=[hbm] * 5,
        out_specs=(pl.BlockSpec(memory_space=vmem),) * 4,
        scratch_shapes=[
            vmem((T, D), BF), vmem((D, S), BF), vmem((2, D, HL), BF), vmem((2, HL, D), BF), vmem((T, D), BF),
            vmem((S, D), BF), vmem((S, T), F32), vmem((S, T), F32), vmem((S, T), BF), vmem((S, T), BF),
            vmem((2, D // 2, T), BF),
            vmem((128, D), BF), vmem((128, D), BF), vmem((128, D), F32),
            vmem((NC, 16, half), BF), vmem((NC, 16, half), BF),
            vmem((128, D + 128), BF), vmem((128, D + 128), BF), vmem((128, D), F32), vmem((S, 128), F32),
            vmem((NC, 16, half), BF), vmem((NC, 16, half), BF),
            vmem((2, 128), F32), vmem((NC, 2, 128), F32), vmem((128, 128), F32),
            vmem((2, HL, D), BF), vmem((2, D, HL), BF),
            vmem((16, half), F32), vmem((NZ, 16, half), BF), vmem((NZ, 16, half), BF),
            vmem((64, D), BF), vmem((64, D), BF), vmem((64, HL), F32),
            vmem((2, 64, HL), BF), vmem((2, 64, HL), BF), vmem((64, D), F32),
            vmem((NZ, 16, half), BF), vmem((NZ, 16, half), BF),
            vmem((NZ, 16, half), BF), vmem((NZ, 16, half), BF),
            vmem((2, NC, 16, half), BF), vmem((2, NC, 16, half + 128), BF), vmem((2, NC, 16, 128), BF),
            vmem((S, D), BF), vmem((S, D), BF),
            vmem((S, T), F32), vmem((S, T), BF), vmem((S, T), BF), vmem((S, T), BF),
            vmem((D // 2, S), BF), vmem((D // 2, S), BF), vmem((D // 2, S), F32),
            vmem((NC, 32, S), BF), vmem((NC, 32, S), BF), vmem((32, S), BF), vmem((NZ, 32, S), BF),
            pltpu.SemaphoreType.DMA((5,)), pltpu.SemaphoreType.DMA((18,)), pltpu.SemaphoreType.DMA((17,)),
            pltpu.SemaphoreType.DMA((NC,)), pltpu.SemaphoreType.DMA((NC,)), pltpu.SemaphoreType.DMA((NC,)),
        ],
        compiler_params=pltpu.CompilerParams(
            collective_id=0, has_side_effects=True, vmem_limit_bytes=36 * 2**20
        ),
        cost_estimate=pl.CostEstimate(flops=4 * 10**9, bytes_accessed=13 * 10**6, transcendentals=10**6),
    )(*(pltpu.with_memory_space_constraint(a, pltpu.HBM) for a in (tokens[0], slot_keys, w_in, w_out, out_grad[0])))
    tg, kg, wig, wog = pl.pallas_call(
        store_kernel,
        out_shape=(
            pltpu.HBM((T, D), BF),
            pltpu.HBM((32, S), F32),
            pltpu.HBM((2, D, HL), BF),
            pltpu.HBM((2, HL, D), BF),
        ),
        in_specs=[pl.BlockSpec(memory_space=vmem)] * 4,
        out_specs=(hbm,) * 4,
        scratch_shapes=[pltpu.SemaphoreType.DMA((4,))],
        compiler_params=pltpu.CompilerParams(vmem_limit_bytes=2**20),
    )(*held)
    return tg[None], kg, wig, wog


def solution(mesh):
    return jax.shard_map(
        per_device,
        mesh=mesh,
        in_specs=(
            P("dp", "ctx", None),
            P(),
            P("ctx", None, "dp"),
            P("ctx", "dp", None),
            P("dp", "ctx", None),
        ),
        out_specs=(
            P("dp", "ctx", None),
            P("ctx", None),
            P("ctx", None, "dp"),
            P("ctx", "dp", None),
        ),
        check_vma=False,
    )
```

```python
import jax
import jax.numpy as jnp
from jax import lax
from jax.experimental import pallas as pl
from jax.experimental.pallas import tpu as pltpu
from jax.sharding import PartitionSpec as P

MESH = pl.DeviceIdType.MESH
BF = jnp.bfloat16
F32 = jnp.float32

T = 640
D = 1024
S = 256
HL = 512
NZ = 8
SIDE = 4
NC = SIDE * SIDE

PLANE = sorted(range(1, NC), key=lambda d: -sum(min(i, SIDE - i) for i in divmod(d, SIDE)))
LINE = sorted(range(1, NZ), key=lambda e: -min(e, NZ - e))

GELU_A = 0.7978845608028654
GELU_B = 0.044715


def gelu_value(value):
    return 0.5 * value * (1.0 + jnp.tanh(GELU_A * (value + GELU_B * value * value * value)))


def gelu_slope(value):
    inner = jnp.tanh(GELU_A * (value + GELU_B * value * value * value))
    return 0.5 * (1.0 + inner) + 0.5 * value * (1.0 - inner * inner) * GELU_A * (
        1.0 + 3.0 * GELU_B * value * value
    )


def nn(a, b):
    return lax.dot_general(a, b, (((1,), (0,)), ((), ())), preferred_element_type=F32)


def nt(a, b):
    return lax.dot_general(a, b, (((1,), (1,)), ((), ())), preferred_element_type=F32)


def tn(a, b):
    return lax.dot_general(a, b, (((0,), (0,)), ((), ())), preferred_element_type=F32)


def fold(rows):
    return jnp.concatenate([rows[:, : D // 2], rows[:, D // 2 :]], axis=0)


def unfold(rows):
    return jnp.concatenate([rows[:8], rows[8:]], axis=1)


def add_all(acc, ref, n):
    for i in range(1, n):
        acc = acc + ref[i].astype(F32)
    return acc


def lanes(shape, columns):
    at = lax.broadcasted_iota(jnp.int32, shape, 1)
    tile = jnp.zeros(shape, F32)
    for i, column in enumerate(columns):
        tile = jnp.where(at == i, column, tile)
    return tile


def split2(value):
    high = value.astype(BF).astype(F32)
    return high, value - high


class Copies:
    def __init__(self, open_copies, make, order, sent, received=None):
        self.make, self.order, self.sent, self.received = make, order, sent, received
        self.to_send = self.to_receive = False
        open_copies.append(self)

    def start(self, d):
        self.to_send = self.to_receive = True
        self.make(d).start()

    def start_all(self):
        for d in self.order:
            self.start(d)

    def wait_recv(self):
        self.to_receive = False
        ref, sem = self.received
        pltpu.make_async_copy(ref, ref, sem).wait()

    def wait_one(self, d):
        self.to_receive = False
        self.make(d).wait_recv()

    def drain(self):
        if self.to_receive:
            if self.received is None:
                for d in self.order:
                    self.wait_one(d)
            else:
                self.wait_recv()
        if self.to_send:
            ref, sem = self.sent
            pltpu.make_async_copy(ref, ref, sem).wait()


class Local:
    def __init__(self, open_copies, *copy):
        self.copy = pltpu.make_async_copy(*copy)
        self.waited = True
        open_copies.append(self)

    def start(self):
        self.waited = False
        self.copy.start()

    def wait(self):
        self.waited = True
        self.copy.wait()

    def drain(self):
        if not self.waited:
            self.wait()


def kernel(
    x_hbm, keys_hbm, wi_hbm, wo_hbm, g_hbm,
    tgs, kout, wigs, wogs,
    x, keys, wi, wo, g,
    keysT, LT, comb, combH, disp, xT,
    gs_send, gs_recv, gsum, gpk, garr,
    us_send, us_recv, usum, ustat, upk, uarr, ust, ustr, utt,
    wiT, woT, rown, zg, zu, gall, rall, pre, act, pg, outp,
    cpk, crecv, bpk, brecv,
    so, si, sm, sof, sif, cpart, lgH, lgN, dispH,
    ks_send, ks_recv, ksum, kpk, karr, kz, kzarr,
    ld, send, recv, do_r, db_r, dm_r,
):
    dp = lax.axis_index("dp")
    ctx = lax.axis_index("ctx")
    core = lax.rem(ctx, 2)
    chip = lax.div(ctx, 2)
    cy, cx = lax.div(chip, SIDE), lax.rem(chip, SIDE)
    other = 1 - core
    sib = {"ctx": chip * 2 + other}

    def ahead(d):
        return lax.rem(cy + d // SIDE, SIDE) * SIDE + lax.rem(cx + d % SIDE, SIDE)

    def behind(d):
        return (
            lax.rem(cy + SIDE - d // SIDE, SIDE) * SIDE
            + lax.rem(cx + SIDE - d % SIDE, SIDE)
        )

    def zahead(e):
        return lax.rem(dp + e, NZ)

    def zbehind(e):
        return lax.rem(dp + NZ - e, NZ)

    open_copies = []

    def remote(src, dst, send, recv, device):
        return pltpu.make_async_remote_copy(
            src_ref=src, dst_ref=dst, send_sem=send, recv_sem=recv,
            device_id=device, device_id_type=MESH,
        )

    load_keys = Local(open_copies, keys_hbm, keys, ld.at[0])
    load_x = Local(open_copies, x_hbm, x, ld.at[1])
    load_g = Local(open_copies, g_hbm, g, ld.at[2])
    load_wo = Local(open_copies, wo_hbm, wo, ld.at[3])
    load_wi = Local(open_copies, wi_hbm, wi, ld.at[4])
    load_keys.start()
    load_x.start()

    barrier = pltpu.get_barrier_semaphore()
    pl.semaphore_signal(barrier, inc=1, device_id=sib, device_id_type=MESH)

    for d in PLANE:
        pl.semaphore_signal(
            barrier, inc=1, device_id={"ctx": ahead(d) * 2 + core}, device_id_type=MESH
        )
    for e in LINE:
        pl.semaphore_signal(barrier, inc=1, device_id={"dp": zahead(e)}, device_id_type=MESH)

    load_keys.wait()
    load_g.start()
    for b in range(D // 128):
        block = keys[b * 128 : (b + 1) * 128, :].astype(F32).T
        keysT[:, b * 128 : (b + 1) * 128] = jnp.concatenate(
            [block[(2 * j + k) * 8 : (2 * j + k) * 8 + 8] for k in range(2) for j in range(NC)], axis=0
        ).astype(BF)
    load_x.wait()
    LT[...] = nt(keysT[...], x[...])
    mine = pl.ds(pl.multiple_of(core * 128, 128), 128)
    theirs = pl.ds(pl.multiple_of(other * 128, 128), 128)
    half = D // 2

    logit = LT[...]
    top = jnp.max(logit, axis=1, keepdims=True).astype(BF).astype(F32)
    e = jnp.exp(logit - top)
    total = jnp.sum(e, axis=1, keepdims=True)
    disp[...] = e.astype(BF)
    high, low = split2(total)
    ustat[...] = lanes((S, 128), (top, high, low))
    us_send[:, :D] = nn(disp[theirs, :], x[...]).astype(BF)
    us_send[:, D:] = ustat[theirs, :].astype(BF)
    pl.semaphore_wait(barrier, NC + NZ - 1)
    sib_u = Copies(
        open_copies, lambda d: remote(us_send, us_recv, send.at[1], recv.at[1], sib), [0],
        (us_send, send.at[1]), (us_recv, recv.at[1]),
    )
    sib_u.start_all()

    for t in range(T // 128):
        at = slice(t * 128, (t + 1) * 128)
        logit = LT[:, at]
        e = jnp.exp(logit - jnp.max(logit, axis=0, keepdims=True))
        e = e / jnp.sum(e, axis=0, keepdims=True)
        comb[:, at] = e
        combH[:, at] = e.astype(BF)
    load_g.wait()
    gs_send[...] = nn(combH[theirs, :], g[...]).astype(BF)
    sib_g = Copies(
        open_copies, lambda d: remote(gs_send, gs_recv, send.at[0], recv.at[0], sib), [0],
        (gs_send, send.at[0]), (gs_recv, recv.at[0]),
    )
    sib_g.start_all()
    usum[...] = nn(disp[mine, :], x[...])

    own = ustat[mine, :]
    sib_u.wait_recv()
    got = us_recv[:, D:].astype(F32)
    top_a, top_b = own[:, 0:1], got[:, 0:1]
    top = jnp.maximum(top_a, top_b)
    wa, wb = jnp.exp(top_a - top), jnp.exp(top_b - top)
    total = (own[:, 1:2] + own[:, 2:3]) * wa + (got[:, 1:2] + got[:, 2:3]) * wb
    usum[...] = usum[...] * wa + us_recv[:, :D].astype(F32) * wb
    ust[...] = lanes((128, 128), (top, total)).T[0:2, :]
    for j in range(NC):
        upk[j] = fold(usum[j * 8 : j * 8 + 8, :]).astype(BF)

    def aw_copy(d):
        return remote(ust, ustr.at[d], send.at[17], recv.at[16], {"ctx": ahead(d) * 2 + core})

    aw = Copies(open_copies, aw_copy, PLANE, (ustr.at[1:NC], send.at[17]), (ustr.at[1:NC], recv.at[16]))
    aw.start_all()

    def au_copy(d):
        j = ahead(d)
        return remote(upk.at[j], uarr.at[d], send.at[4], recv.at[4], {"ctx": j * 2 + core})

    au = Copies(open_copies, au_copy, PLANE, (upk.at[0 : NC - 1], send.at[4]), (uarr.at[1:NC], recv.at[4]))
    au.start_all()
    uarr[0] = upk[chip]
    ustr[0] = ust[...]

    gsum[...] = nn(combH[mine, :], g[...])
    sib_g.wait_recv()
    gsum[...] += gs_recv[...].astype(F32)

    def ag_copy(d):
        j = ahead(d)
        return remote(gpk.at[j], garr.at[d], send.at[3], recv.at[3], {"ctx": j * 2 + core})

    ag = Copies(open_copies, ag_copy, PLANE, (gpk.at[0 : NC - 1], send.at[3]), (garr.at[1:NC], recv.at[3]))
    for j in range(NC):
        gpk[j] = fold(gsum[j * 8 : j * 8 + 8, :]).astype(BF)
    ag.start_all()
    load_wi.start()
    load_wo.start()

    for b in range(D // 128):
        block = x[:, b * 128 : (b + 1) * 128].T
        xT[0, b * 64 : (b + 1) * 64, :] = jnp.concatenate([block[0:32], block[64:96]], axis=0)
        xT[1, b * 64 : (b + 1) * 64, :] = jnp.concatenate([block[32:64], block[96:128]], axis=0)

    load_wi.wait()
    load_wo.wait()
    for e in range(2):
        for b in range(D // 128):
            at = slice(b * 128, (b + 1) * 128)
            wiT[e, :, at] = wi[e, at, :].T
        for b in range(HL // 128):
            at = slice(b * 128, (b + 1) * 128)
            woT[e, :, at] = wo[e, at, :].T

    au.wait_recv()
    aw.wait_recv()
    utt[...] = jnp.concatenate(
        [ustr[:, 0, :], ustr[:, 1, :], jnp.zeros((128 - 2 * NC, 128), F32)], axis=0
    ).T
    stats = utt[pl.ds(pl.multiple_of(chip * 8, 8), 8), :]
    stats = jnp.concatenate([stats, stats], axis=0)
    top = jnp.max(stats[:, :NC], axis=1, keepdims=True)
    w = jnp.exp(stats[:, :NC] - top)
    total = jnp.sum(w * stats[:, NC : 2 * NC], axis=1, keepdims=True)
    acc = jnp.zeros((16, half), F32)
    for d in range(NC):
        acc = acc + w[:, d : d + 1] * uarr[d].astype(F32)
    acc = acc / total
    rown[...] = acc
    zu[dp] = acc.astype(BF)

    def bu_copy(e):
        return remote(zu.at[dp], zu.at[dp], send.at[6], recv.at[6], {"dp": zahead(e)})

    bu = Copies(open_copies, bu_copy, LINE, (zu.at[0 : NZ - 1], send.at[6]), (zu.at[0 : NZ - 1], recv.at[6]))
    bu.start_all()
    z_high, z_low = split2(total)
    sm[core, chip] = lanes((16, 128), (top, z_high, z_low)).astype(BF)

    acc = fold(gsum[pl.ds(pl.multiple_of(chip * 8, 8), 8), :])
    ag.wait_recv()
    zg[dp] = add_all(acc, garr, NC).astype(BF)

    def bg_copy(e):
        return remote(zg.at[dp], zg.at[dp], send.at[5], recv.at[5], {"dp": zahead(e)})

    bg = Copies(open_copies, bg_copy, LINE, (zg.at[0 : NZ - 1], send.at[5]), (zg.at[0 : NZ - 1], recv.at[5]))
    bg.start_all()

    def dm_copy(d):
        return remote(
            sm.at[core, chip], sm.at[core, chip], send.at[15], dm_r.at[d], {"ctx": ahead(d) * 2 + core}
        )

    def fm_copy(d):
        j = behind(d)
        return remote(sm.at[core, j], sm.at[core, j], send.at[16], recv.at[15], sib)

    dm = Copies(open_copies, dm_copy, PLANE, (sm.at[0, 0 : NC - 1], send.at[15]))
    fm = Copies(open_copies, fm_copy, [], (sm.at[0], send.at[16]), (sm.at[0], recv.at[15]))
    dm.start_all()
    fm.start(0)

    first = lax.rem(lax.broadcasted_iota(jnp.int32, (64, HL), 0), 8) < 4
    bu.wait_recv()
    rall[...] = jnp.concatenate([unfold(zu[c].astype(F32)) for c in range(NZ)], axis=0).astype(BF)
    pre_act = jnp.where(first, nn(rall[...], wi[0]), nn(rall[...], wi[1]))
    a = gelu_value(pre_act)
    act[0] = jnp.where(first, a, 0.0).astype(BF)
    act[1] = jnp.where(first, 0.0, a).astype(BF)
    pre[...] = gelu_slope(pre_act)
    outp[...] = nn(act[0], wo[0]) + nn(act[1], wo[1])

    def co_copy(e):
        j = zahead(e)
        return remote(cpk.at[j], crecv.at[e], send.at[7], recv.at[7], {"dp": j})

    co = Copies(open_copies, co_copy, LINE, (cpk.at[0 : NZ - 1], send.at[7]), (crecv.at[1:NZ], recv.at[7]))
    for j in range(NZ):
        cpk[j] = fold(outp[j * 8 : j * 8 + 8, :]).astype(BF)
    co.start_all()
    o_own = fold(outp[pl.ds(pl.multiple_of(dp * 8, 8), 8), :])

    bg.wait_recv()
    gall[...] = jnp.concatenate([unfold(zg[c].astype(F32)) for c in range(NZ)], axis=0).astype(BF)
    p = jnp.where(first, nn(gall[...], woT[0]), nn(gall[...], woT[1])) * pre[...]
    pg[0] = jnp.where(first, p, 0.0).astype(BF)
    pg[1] = jnp.where(first, 0.0, p).astype(BF)
    outp[...] = nn(pg[0], wiT[0]) + nn(pg[1], wiT[1])

    def cb_copy(e):
        j = zahead(e)
        return remote(bpk.at[j], brecv.at[e], send.at[8], recv.at[8], {"dp": j})

    cb = Copies(open_copies, cb_copy, LINE, (bpk.at[0 : NZ - 1], send.at[8]), (brecv.at[1:NZ], recv.at[8]))
    for j in range(NZ):
        bpk[j] = fold(outp[j * 8 : j * 8 + 8, :]).astype(BF)
    cb.start_all()
    b_own = fold(outp[pl.ds(pl.multiple_of(dp * 8, 8), 8), :])

    for d in reversed(PLANE):
        dm.wait_one(d)
        fm.start(d)

    co.wait_recv()
    so[core, chip] = add_all(o_own, crecv, NZ).astype(BF)

    def do_copy(d):
        return remote(
            so.at[core, chip], so.at[core, chip], send.at[9], do_r.at[d], {"ctx": ahead(d) * 2 + core}
        )

    def fo_copy(d):
        j = behind(d)
        return remote(so.at[core, j], so.at[core, j], send.at[11], recv.at[11], sib)

    do = Copies(open_copies, do_copy, PLANE, (so.at[0, 0 : NC - 1], send.at[9]))
    fo = Copies(open_copies, fo_copy, [], (so.at[0], send.at[11]), (so.at[0], recv.at[11]))
    do.start_all()
    fo.start(0)

    for e in range(2):
        for c in range(HL // 128):
            at = slice(c * 128, (c + 1) * 128)
            wogs[e, at, :] = tn(act[e, :, at], gall[...]).astype(BF)

    def stat_of(ref, low):
        return jnp.concatenate(
            [ref[k, j, 0:8, low : low + 128].astype(F32) for k in range(2) for j in range(NC)], axis=0
        )

    fm.wait_recv()
    stat = stat_of(sm, 0)
    top = stat[:, 0:1]
    over = 1.0 / (stat[:, 1:2] + stat[:, 2:3])
    for t in range(T // 128):
        at = slice(t * 128, (t + 1) * 128)
        prob = jnp.exp(LT[:, at] - top) * over
        LT[:, at] = prob
        dispH[:, at] = prob.astype(BF)

    cb.wait_recv()
    back = add_all(b_own, brecv, NZ).astype(BF)
    si[core, chip, :, :half] = back
    inner = jnp.sum(rown[...] * back.astype(F32), axis=1, keepdims=True)
    inner = inner[:8] + inner[8:]
    inner = jnp.concatenate([inner, inner], axis=0)
    i_high, i_low = split2(inner)
    si[core, chip, :, half:] = lanes((16, 128), (i_high, i_low)).astype(BF)

    def db_copy(d):
        return remote(
            si.at[core, chip], si.at[core, chip], send.at[10], db_r.at[d], {"ctx": ahead(d) * 2 + core}
        )

    def fb_copy(d):
        j = behind(d)
        return remote(si.at[core, j], si.at[core, j], send.at[12], recv.at[12], sib)

    db = Copies(open_copies, db_copy, PLANE, (si.at[0, 0 : NC - 1], send.at[10]))
    fb = Copies(open_copies, fb_copy, [], (si.at[0], send.at[12]), (si.at[0], recv.at[12]))
    db.start_all()
    fb.start(0)
    for e in range(2):
        for c in range(D // 128):
            at = slice(c * 128, (c + 1) * 128)
            wigs[e, at, :] = tn(rall[:, at], pg[e]).astype(BF)

    def gather(ref, rows, k):
        for q in range(NC // 2):
            rows[pl.ds(pl.multiple_of(k * 128 + q * 16, 16), 16), :] = jnp.concatenate(
                [unfold(ref[k, 2 * q + i, :, :half].astype(F32)) for i in range(2)], axis=0
            ).astype(BF)

    for d in reversed(PLANE):
        do.wait_one(d)
        fo.start(d)
    gather(so, sof, core)
    cpart[mine, :] = nt(sof[mine, :], g[...])
    fo.wait_recv()
    gather(so, sof, other)
    cpart[theirs, :] = nt(sof[theirs, :], g[...])
    for t in range(T // 128):
        at = slice(t * 128, (t + 1) * 128)
        prob, back = comb[:, at], cpart[:, at]
        cpart[:, at] = prob * (back - jnp.sum(prob * back, axis=0, keepdims=True))
    for d in reversed(PLANE):
        db.wait_one(d)
        fb.start(d)
    gather(si, sif, core)
    comb[mine, :] = nt(sif[mine, :], x[...])
    fb.wait_recv()
    gather(si, sif, other)
    comb[theirs, :] = nt(sif[theirs, :], x[...])
    stat = stat_of(si, half)
    inner = stat[:, 0:1] + stat[:, 1:2]
    for t in range(T // 128):
        at = slice(t * 128, (t + 1) * 128)
        lg = LT[:, at] * (comb[:, at] - inner) + cpart[:, at]
        lgH[:, at] = lg.astype(BF)
        lgN[:, at] = jnp.concatenate(
            [lg[k * 128 + j * 8 : k * 128 + j * 8 + 8] for j in range(NC) for k in range(2)], axis=0
        ).astype(BF)

    ks_send[...] = nt(xT[other], lgN[...]).astype(BF)
    sib_k = Copies(
        open_copies, lambda d: remote(ks_send, ks_recv, send.at[2], recv.at[2], sib), [0],
        (ks_send, send.at[2]), (ks_recv, recv.at[2]),
    )
    sib_k.start_all()
    ksum[...] = nt(xT[core], lgN[...])
    sib_k.wait_recv()
    ksum[...] += ks_recv[...].astype(F32)

    def fk_copy(d):
        j = ahead(d)
        return remote(kpk.at[j], karr.at[d], send.at[13], recv.at[13], {"ctx": j * 2 + core})

    fk = Copies(open_copies, fk_copy, PLANE, (kpk.at[0 : NC - 1], send.at[13]), (karr.at[1:NC], recv.at[13]))

    for j in range(NC):
        kpk[j] = ksum[j * 32 : j * 32 + 32, :].astype(BF)
    fk.start_all()

    for t in range(T // 128):
        at = slice(t * 128, (t + 1) * 128)
        tgs[at, :] = (tn(lgH[:, at], keysT[...]) + tn(dispH[:, at], sif[...])).astype(BF)

    fk.wait_recv()
    acc = add_all(ksum[pl.ds(pl.multiple_of(chip * 32, 32), 32), :], karr, NC)
    kz[...] = acc.astype(BF)

    def fz_copy(e):
        return remote(kz, kzarr.at[e], send.at[14], recv.at[14], {"dp": zahead(e)})

    fz = Copies(open_copies, fz_copy, LINE, (kzarr.at[0 : NZ - 1], send.at[14]), (kzarr.at[1:NZ], recv.at[14]))


    fz.start_all()

    fz.wait_recv()
    kout[...] = add_all(acc, kzarr, NZ)

    for copies in open_copies:
        copies.drain()


def store_kernel(tgs, kout, wigs, wogs, tg_hbm, kg_hbm, wig_hbm, wog_hbm, st):
    pairs = ((wigs, wig_hbm), (wogs, wog_hbm), (tgs, tg_hbm), (kout, kg_hbm))
    copies = [pltpu.make_async_copy(src, dst, st.at[i]) for i, (src, dst) in enumerate(pairs)]
    for copy in copies:
        copy.start()
    for copy in copies:
        copy.wait()


def per_device(tokens, slot_keys, w_in, w_out, out_grad):
    hbm = pl.BlockSpec(memory_space=pltpu.HBM)
    vmem = pltpu.VMEM
    half = D // 2
    held = pl.pallas_call(
        kernel,
        out_shape=(
            pltpu.VMEM((T, D), BF),
            pltpu.VMEM((32, S), F32),
            pltpu.VMEM((2, D, HL), BF),
            pltpu.VMEM((2, HL, D), BF),
        ),
        in_specs=[hbm] * 5,
        out_specs=(pl.BlockSpec(memory_space=vmem),) * 4,
        scratch_shapes=[
            vmem((T, D), BF), vmem((D, S), BF), vmem((2, D, HL), BF), vmem((2, HL, D), BF), vmem((T, D), BF),
            vmem((S, D), BF), vmem((S, T), F32), vmem((S, T), F32), vmem((S, T), BF), vmem((S, T), BF),
            vmem((2, D // 2, T), BF),
            vmem((128, D), BF), vmem((128, D), BF), vmem((128, D), F32),
            vmem((NC, 16, half), BF), vmem((NC, 16, half), BF),
            vmem((128, D + 128), BF), vmem((128, D + 128), BF), vmem((128, D), F32), vmem((S, 128), F32),
            vmem((NC, 16, half), BF), vmem((NC, 16, half), BF),
            vmem((2, 128), F32), vmem((NC, 2, 128), F32), vmem((128, 128), F32),
            vmem((2, HL, D), BF), vmem((2, D, HL), BF),
            vmem((16, half), F32), vmem((NZ, 16, half), BF), vmem((NZ, 16, half), BF),
            vmem((64, D), BF), vmem((64, D), BF), vmem((64, HL), F32),
            vmem((2, 64, HL), BF), vmem((2, 64, HL), BF), vmem((64, D), F32),
            vmem((NZ, 16, half), BF), vmem((NZ, 16, half), BF),
            vmem((NZ, 16, half), BF), vmem((NZ, 16, half), BF),
            vmem((2, NC, 16, half), BF), vmem((2, NC, 16, half + 128), BF), vmem((2, NC, 16, 128), BF),
            vmem((S, D), BF), vmem((S, D), BF),
            vmem((S, T), F32), vmem((S, T), BF), vmem((S, T), BF), vmem((S, T), BF),
            vmem((D // 2, S), BF), vmem((D // 2, S), BF), vmem((D // 2, S), F32),
            vmem((NC, 32, S), BF), vmem((NC, 32, S), BF), vmem((32, S), BF), vmem((NZ, 32, S), BF),
            pltpu.SemaphoreType.DMA((5,)), pltpu.SemaphoreType.DMA((18,)), pltpu.SemaphoreType.DMA((17,)),
            pltpu.SemaphoreType.DMA((NC,)), pltpu.SemaphoreType.DMA((NC,)), pltpu.SemaphoreType.DMA((NC,)),
        ],
        compiler_params=pltpu.CompilerParams(
            collective_id=0, has_side_effects=True, vmem_limit_bytes=36 * 2**20
        ),
        cost_estimate=pl.CostEstimate(flops=4 * 10**9, bytes_accessed=13 * 10**6, transcendentals=10**6),
    )(*(pltpu.with_memory_space_constraint(a, pltpu.HBM) for a in (tokens[0], slot_keys, w_in, w_out, out_grad[0])))
    tg, kg, wig, wog = pl.pallas_call(
        store_kernel,
        out_shape=(
            pltpu.HBM((T, D), BF),
            pltpu.HBM((32, S), F32),
            pltpu.HBM((2, D, HL), BF),
            pltpu.HBM((2, HL, D), BF),
        ),
        in_specs=[pl.BlockSpec(memory_space=vmem)] * 4,
        out_specs=(hbm,) * 4,
        scratch_shapes=[pltpu.SemaphoreType.DMA((4,))],
        compiler_params=pltpu.CompilerParams(vmem_limit_bytes=2**20),
    )(*held)
    return tg[None], kg, wig, wog


def solution(mesh):
    return jax.shard_map(
        per_device,
        mesh=mesh,
        in_specs=(
            P("dp", "ctx", None),
            P(),
            P("ctx", None, "dp"),
            P("ctx", "dp", None),
            P("dp", "ctx", None),
        ),
        out_specs=(
            P("dp", "ctx", None),
            P("ctx", None),
            P("ctx", None, "dp"),
            P("ctx", "dp", None),
        ),
        check_vma=False,
    )
```

```python
import jax
import jax.numpy as jnp
from jax import lax
from jax.experimental import pallas as pl
from jax.experimental.pallas import tpu as pltpu
from jax.sharding import PartitionSpec as P

MESH = pl.DeviceIdType.MESH
BF = jnp.bfloat16
F32 = jnp.float32

T = 640
D = 1024
S = 256
HL = 512
NZ = 8
SIDE = 4
NC = SIDE * SIDE

PLANE = sorted(range(1, NC), key=lambda d: -sum(min(i, SIDE - i) for i in divmod(d, SIDE)))
LINE = sorted(range(1, NZ), key=lambda e: -min(e, NZ - e))

GELU_A = 0.7978845608028654
GELU_B = 0.044715


def gelu_value(value):
    return 0.5 * value * (1.0 + jnp.tanh(GELU_A * (value + GELU_B * value * value * value)))


def gelu_slope(value):
    inner = jnp.tanh(GELU_A * (value + GELU_B * value * value * value))
    return 0.5 * (1.0 + inner) + 0.5 * value * (1.0 - inner * inner) * GELU_A * (
        1.0 + 3.0 * GELU_B * value * value
    )


def nn(a, b):
    return lax.dot_general(a, b, (((1,), (0,)), ((), ())), preferred_element_type=F32)


def nt(a, b):
    return lax.dot_general(a, b, (((1,), (1,)), ((), ())), preferred_element_type=F32)


def tn(a, b):
    return lax.dot_general(a, b, (((0,), (0,)), ((), ())), preferred_element_type=F32)


def fold(rows):
    return jnp.concatenate([rows[:, : D // 2], rows[:, D // 2 :]], axis=0)


def unfold(rows):
    return jnp.concatenate([rows[:8], rows[8:]], axis=1)


def add_all(acc, ref, n):
    for i in range(1, n):
        acc = acc + ref[i].astype(F32)
    return acc


def lanes(shape, columns):
    at = lax.broadcasted_iota(jnp.int32, shape, 1)
    tile = jnp.zeros(shape, F32)
    for i, column in enumerate(columns):
        tile = jnp.where(at == i, column, tile)
    return tile


def split2(value):
    high = value.astype(BF).astype(F32)
    return high, value - high


class Copies:
    def __init__(self, open_copies, make, order, sent, received=None):
        self.make, self.order, self.sent, self.received = make, order, sent, received
        self.to_send = self.to_receive = False
        open_copies.append(self)

    def start(self, d):
        self.to_send = self.to_receive = True
        self.make(d).start()

    def start_all(self):
        for d in self.order:
            self.start(d)

    def wait_recv(self):
        self.to_receive = False
        ref, sem = self.received
        pltpu.make_async_copy(ref, ref, sem).wait()

    def wait_one(self, d):
        self.to_receive = False
        self.make(d).wait_recv()

    def drain(self):
        if self.to_receive:
            if self.received is None:
                for d in self.order:
                    self.wait_one(d)
            else:
                self.wait_recv()
        if self.to_send:
            self.to_send = False
            ref, sem = self.sent
            pltpu.make_async_copy(ref, ref, sem).wait()


class Local:
    def __init__(self, open_copies, *copy):
        self.copy = pltpu.make_async_copy(*copy)
        self.waited = True
        open_copies.append(self)

    def start(self):
        self.waited = False
        self.copy.start()

    def wait(self):
        self.waited = True
        self.copy.wait()

    def drain(self):
        if not self.waited:
            self.wait()


def kernel(
    x_hbm, keys_hbm, wi_hbm, wo_hbm, g_hbm,
    tgs, kout, wigs, wogs,
    x, keys, wi, wo, g,
    keysT, LT, comb, combH, disp, xT,
    gs_send, gs_recv, gsum, gpk, garr,
    us_send, us_recv, usum, ustat, upk, uarr, ust, ustr, utt,
    wiT, woT, rown, zg, zu, gall, rall, pre, act, pg, outp,
    cpk, crecv, bpk, brecv,
    so, si, sm, sof, sif, cpart, lgH, lgN, dispH,
    ks_send, ks_recv, ksum, kpk, karr, kz, kzarr,
    ld, send, recv, do_r, db_r, dm_r,
):
    dp = lax.axis_index("dp")
    ctx = lax.axis_index("ctx")
    core = lax.rem(ctx, 2)
    chip = lax.div(ctx, 2)
    cy, cx = lax.div(chip, SIDE), lax.rem(chip, SIDE)
    other = 1 - core
    sib = {"ctx": chip * 2 + other}

    def ahead(d):
        return lax.rem(cy + d // SIDE, SIDE) * SIDE + lax.rem(cx + d % SIDE, SIDE)

    def behind(d):
        return (
            lax.rem(cy + SIDE - d // SIDE, SIDE) * SIDE
            + lax.rem(cx + SIDE - d % SIDE, SIDE)
        )

    def zahead(e):
        return lax.rem(dp + e, NZ)

    def zbehind(e):
        return lax.rem(dp + NZ - e, NZ)

    open_copies = []

    def remote(src, dst, send, recv, device):
        return pltpu.make_async_remote_copy(
            src_ref=src, dst_ref=dst, send_sem=send, recv_sem=recv,
            device_id=device, device_id_type=MESH,
        )

    load_keys = Local(open_copies, keys_hbm, keys, ld.at[0])
    load_x = Local(open_copies, x_hbm, x, ld.at[1])
    load_g = Local(open_copies, g_hbm, g, ld.at[2])
    load_wo = Local(open_copies, wo_hbm, wo, ld.at[3])
    load_wi = Local(open_copies, wi_hbm, wi, ld.at[4])
    load_keys.start()
    load_x.start()

    barrier = pltpu.get_barrier_semaphore()
    pl.semaphore_signal(barrier, inc=1, device_id=sib, device_id_type=MESH)

    for d in PLANE:
        pl.semaphore_signal(
            barrier, inc=1, device_id={"ctx": ahead(d) * 2 + core}, device_id_type=MESH
        )
    for e in LINE:
        pl.semaphore_signal(barrier, inc=1, device_id={"dp": zahead(e)}, device_id_type=MESH)

    load_keys.wait()
    load_g.start()
    for b in range(D // 128):
        block = keys[b * 128 : (b + 1) * 128, :].astype(F32).T
        keysT[:, b * 128 : (b + 1) * 128] = jnp.concatenate(
            [block[(2 * j + k) * 8 : (2 * j + k) * 8 + 8] for k in range(2) for j in range(NC)], axis=0
        ).astype(BF)
    load_x.wait()
    LT[...] = nt(keysT[...], x[...])
    mine = pl.ds(pl.multiple_of(core * 128, 128), 128)
    theirs = pl.ds(pl.multiple_of(other * 128, 128), 128)
    half = D // 2

    logit = LT[...]
    top = jnp.max(logit, axis=1, keepdims=True).astype(BF).astype(F32)
    e = jnp.exp(logit - top)
    total = jnp.sum(e, axis=1, keepdims=True)
    disp[...] = e.astype(BF)
    high, low = split2(total)
    ustat[...] = lanes((S, 128), (top, high, low))
    us_send[:, :D] = nn(disp[theirs, :], x[...]).astype(BF)
    us_send[:, D:] = ustat[theirs, :].astype(BF)
    pl.semaphore_wait(barrier, NC + NZ - 1)
    sib_u = Copies(
        open_copies, lambda d: remote(us_send, us_recv, send.at[1], recv.at[1], sib), [0],
        (us_send, send.at[1]), (us_recv, recv.at[1]),
    )
    sib_u.start_all()

    for t in range(T // 128):
        at = slice(t * 128, (t + 1) * 128)
        logit = LT[:, at]
        e = jnp.exp(logit - jnp.max(logit, axis=0, keepdims=True))
        e = e / jnp.sum(e, axis=0, keepdims=True)
        comb[:, at] = e
        combH[:, at] = e.astype(BF)
    load_g.wait()
    gs_send[...] = nn(combH[theirs, :], g[...]).astype(BF)
    sib_g = Copies(
        open_copies, lambda d: remote(gs_send, gs_recv, send.at[0], recv.at[0], sib), [0],
        (gs_send, send.at[0]), (gs_recv, recv.at[0]),
    )
    sib_g.start_all()
    usum[...] = nn(disp[mine, :], x[...])

    own = ustat[mine, :]
    sib_u.wait_recv()
    got = us_recv[:, D:].astype(F32)
    top_a, top_b = own[:, 0:1], got[:, 0:1]
    top = jnp.maximum(top_a, top_b)
    wa, wb = jnp.exp(top_a - top), jnp.exp(top_b - top)
    total = (own[:, 1:2] + own[:, 2:3]) * wa + (got[:, 1:2] + got[:, 2:3]) * wb
    usum[...] = usum[...] * wa + us_recv[:, :D].astype(F32) * wb
    ust[...] = lanes((128, 128), (top, total)).T[0:2, :]
    for j in range(NC):
        upk[j] = fold(usum[j * 8 : j * 8 + 8, :]).astype(BF)

    def aw_copy(d):
        return remote(ust, ustr.at[d], send.at[17], recv.at[16], {"ctx": ahead(d) * 2 + core})

    aw = Copies(open_copies, aw_copy, PLANE, (ustr.at[1:NC], send.at[17]), (ustr.at[1:NC], recv.at[16]))
    aw.start_all()

    def au_copy(d):
        j = ahead(d)
        return remote(upk.at[j], uarr.at[d], send.at[4], recv.at[4], {"ctx": j * 2 + core})

    au = Copies(open_copies, au_copy, PLANE, (upk.at[0 : NC - 1], send.at[4]), (uarr.at[1:NC], recv.at[4]))
    au.start_all()
    uarr[0] = upk[chip]
    ustr[0] = ust[...]

    gsum[...] = nn(combH[mine, :], g[...])
    sib_g.wait_recv()
    gsum[...] += gs_recv[...].astype(F32)

    def ag_copy(d):
        j = ahead(d)
        return remote(gpk.at[j], garr.at[d], send.at[3], recv.at[3], {"ctx": j * 2 + core})

    ag = Copies(open_copies, ag_copy, PLANE, (gpk.at[0 : NC - 1], send.at[3]), (garr.at[1:NC], recv.at[3]))
    for j in range(NC):
        gpk[j] = fold(gsum[j * 8 : j * 8 + 8, :]).astype(BF)
    ag.start_all()
    load_wi.start()
    load_wo.start()

    for b in range(D // 128):
        block = x[:, b * 128 : (b + 1) * 128].T
        xT[0, b * 64 : (b + 1) * 64, :] = jnp.concatenate([block[0:32], block[64:96]], axis=0)
        xT[1, b * 64 : (b + 1) * 64, :] = jnp.concatenate([block[32:64], block[96:128]], axis=0)

    load_wi.wait()
    load_wo.wait()
    for e in range(2):
        for b in range(D // 128):
            at = slice(b * 128, (b + 1) * 128)
            wiT[e, :, at] = wi[e, at, :].T
        for b in range(HL // 128):
            at = slice(b * 128, (b + 1) * 128)
            woT[e, :, at] = wo[e, at, :].T

    au.wait_recv()
    aw.wait_recv()
    utt[...] = jnp.concatenate(
        [ustr[:, 0, :], ustr[:, 1, :], jnp.zeros((128 - 2 * NC, 128), F32)], axis=0
    ).T
    stats = utt[pl.ds(pl.multiple_of(chip * 8, 8), 8), :]
    stats = jnp.concatenate([stats, stats], axis=0)
    top = jnp.max(stats[:, :NC], axis=1, keepdims=True)
    w = jnp.exp(stats[:, :NC] - top)
    total = jnp.sum(w * stats[:, NC : 2 * NC], axis=1, keepdims=True)
    acc = jnp.zeros((16, half), F32)
    for d in range(NC):
        acc = acc + w[:, d : d + 1] * uarr[d].astype(F32)
    acc = acc / total
    rown[...] = acc
    zu[dp] = acc.astype(BF)

    def bu_copy(e):
        return remote(zu.at[dp], zu.at[dp], send.at[6], recv.at[6], {"dp": zahead(e)})

    bu = Copies(open_copies, bu_copy, LINE, (zu.at[0 : NZ - 1], send.at[6]), (zu.at[0 : NZ - 1], recv.at[6]))
    bu.start_all()
    z_high, z_low = split2(total)
    sm[core, chip] = lanes((16, 128), (top, z_high, z_low)).astype(BF)

    acc = fold(gsum[pl.ds(pl.multiple_of(chip * 8, 8), 8), :])
    ag.wait_recv()
    zg[dp] = add_all(acc, garr, NC).astype(BF)

    def bg_copy(e):
        return remote(zg.at[dp], zg.at[dp], send.at[5], recv.at[5], {"dp": zahead(e)})

    bg = Copies(open_copies, bg_copy, LINE, (zg.at[0 : NZ - 1], send.at[5]), (zg.at[0 : NZ - 1], recv.at[5]))
    bg.start_all()

    def dm_copy(d):
        return remote(
            sm.at[core, chip], sm.at[core, chip], send.at[15], dm_r.at[d], {"ctx": ahead(d) * 2 + core}
        )

    def fm_copy(d):
        j = behind(d)
        return remote(sm.at[core, j], sm.at[core, j], send.at[16], recv.at[15], sib)

    dm = Copies(open_copies, dm_copy, PLANE, (sm.at[0, 0 : NC - 1], send.at[15]))
    fm = Copies(open_copies, fm_copy, [], (sm.at[0], send.at[16]), (sm.at[0], recv.at[15]))
    dm.start_all()
    fm.start(0)

    first = lax.rem(lax.broadcasted_iota(jnp.int32, (64, HL), 0), 8) < 4
    bu.wait_recv()
    rall[...] = jnp.concatenate([unfold(zu[c].astype(F32)) for c in range(NZ)], axis=0).astype(BF)
    pre_act = jnp.where(first, nn(rall[...], wi[0]), nn(rall[...], wi[1]))
    a = gelu_value(pre_act)
    act[0] = jnp.where(first, a, 0.0).astype(BF)
    act[1] = jnp.where(first, 0.0, a).astype(BF)
    pre[...] = gelu_slope(pre_act)
    outp[...] = nn(act[0], wo[0]) + nn(act[1], wo[1])

    def co_copy(e):
        j = zahead(e)
        return remote(cpk.at[j], crecv.at[e], send.at[7], recv.at[7], {"dp": j})

    co = Copies(open_copies, co_copy, LINE, (cpk.at[0 : NZ - 1], send.at[7]), (crecv.at[1:NZ], recv.at[7]))
    for j in range(NZ):
        cpk[j] = fold(outp[j * 8 : j * 8 + 8, :]).astype(BF)
    co.start_all()
    o_own = fold(outp[pl.ds(pl.multiple_of(dp * 8, 8), 8), :])

    bg.wait_recv()
    gall[...] = jnp.concatenate([unfold(zg[c].astype(F32)) for c in range(NZ)], axis=0).astype(BF)
    p = jnp.where(first, nn(gall[...], woT[0]), nn(gall[...], woT[1])) * pre[...]
    pg[0] = jnp.where(first, p, 0.0).astype(BF)
    pg[1] = jnp.where(first, 0.0, p).astype(BF)
    outp[...] = nn(pg[0], wiT[0]) + nn(pg[1], wiT[1])

    def cb_copy(e):
        j = zahead(e)
        return remote(bpk.at[j], brecv.at[e], send.at[8], recv.at[8], {"dp": j})

    cb = Copies(open_copies, cb_copy, LINE, (bpk.at[0 : NZ - 1], send.at[8]), (brecv.at[1:NZ], recv.at[8]))
    for j in range(NZ):
        bpk[j] = fold(outp[j * 8 : j * 8 + 8, :]).astype(BF)
    cb.start_all()
    b_own = fold(outp[pl.ds(pl.multiple_of(dp * 8, 8), 8), :])

    for d in reversed(PLANE):
        dm.wait_one(d)
        fm.start(d)

    co.wait_recv()
    so[core, chip] = add_all(o_own, crecv, NZ).astype(BF)

    def do_copy(d):
        return remote(
            so.at[core, chip], so.at[core, chip], send.at[9], do_r.at[d], {"ctx": ahead(d) * 2 + core}
        )

    def fo_copy(d):
        j = behind(d)
        return remote(so.at[core, j], so.at[core, j], send.at[11], recv.at[11], sib)

    do = Copies(open_copies, do_copy, PLANE, (so.at[0, 0 : NC - 1], send.at[9]))
    fo = Copies(open_copies, fo_copy, [], (so.at[0], send.at[11]), (so.at[0], recv.at[11]))
    do.start_all()
    fo.start(0)

    for e in range(2):
        for c in range(HL // 128):
            at = slice(c * 128, (c + 1) * 128)
            wogs[e, at, :] = tn(act[e, :, at], gall[...]).astype(BF)

    def stat_of(ref, low):
        return jnp.concatenate(
            [ref[k, j, 0:8, low : low + 128].astype(F32) for k in range(2) for j in range(NC)], axis=0
        )

    fm.wait_recv()
    stat = stat_of(sm, 0)
    top = stat[:, 0:1]
    over = 1.0 / (stat[:, 1:2] + stat[:, 2:3])
    for t in range(T // 128):
        at = slice(t * 128, (t + 1) * 128)
        prob = jnp.exp(LT[:, at] - top) * over
        LT[:, at] = prob
        dispH[:, at] = prob.astype(BF)

    cb.wait_recv()
    back = add_all(b_own, brecv, NZ).astype(BF)
    si[core, chip, :, :half] = back
    inner = jnp.sum(rown[...] * back.astype(F32), axis=1, keepdims=True)
    inner = inner[:8] + inner[8:]
    inner = jnp.concatenate([inner, inner], axis=0)
    i_high, i_low = split2(inner)
    si[core, chip, :, half:] = lanes((16, 128), (i_high, i_low)).astype(BF)

    def db_copy(d):
        return remote(
            si.at[core, chip], si.at[core, chip], send.at[10], db_r.at[d], {"ctx": ahead(d) * 2 + core}
        )

    def fb_copy(d):
        j = behind(d)
        return remote(si.at[core, j], si.at[core, j], send.at[12], recv.at[12], sib)

    db = Copies(open_copies, db_copy, PLANE, (si.at[0, 0 : NC - 1], send.at[10]))
    fb = Copies(open_copies, fb_copy, [], (si.at[0], send.at[12]), (si.at[0], recv.at[12]))
    db.start_all()
    fb.start(0)
    for e in range(2):
        for c in range(D // 128):
            at = slice(c * 128, (c + 1) * 128)
            wigs[e, at, :] = tn(rall[:, at], pg[e]).astype(BF)

    def gather(ref, rows, k):
        for q in range(NC // 2):
            rows[pl.ds(pl.multiple_of(k * 128 + q * 16, 16), 16), :] = jnp.concatenate(
                [unfold(ref[k, 2 * q + i, :, :half].astype(F32)) for i in range(2)], axis=0
            ).astype(BF)

    for d in reversed(PLANE):
        do.wait_one(d)
        fo.start(d)
    gather(so, sof, core)
    cpart[mine, :] = nt(sof[mine, :], g[...])
    fo.wait_recv()
    gather(so, sof, other)
    cpart[theirs, :] = nt(sof[theirs, :], g[...])
    for t in range(T // 128):
        at = slice(t * 128, (t + 1) * 128)
        prob, back = comb[:, at], cpart[:, at]
        cpart[:, at] = prob * (back - jnp.sum(prob * back, axis=0, keepdims=True))
    for d in reversed(PLANE):
        db.wait_one(d)
        fb.start(d)
    gather(si, sif, core)
    comb[mine, :] = nt(sif[mine, :], x[...])
    fb.wait_recv()
    gather(si, sif, other)
    comb[theirs, :] = nt(sif[theirs, :], x[...])
    stat = stat_of(si, half)
    inner = stat[:, 0:1] + stat[:, 1:2]
    for t in range(T // 128):
        at = slice(t * 128, (t + 1) * 128)
        lg = LT[:, at] * (comb[:, at] - inner) + cpart[:, at]
        lgH[:, at] = lg.astype(BF)
        lgN[:, at] = jnp.concatenate(
            [lg[k * 128 + j * 8 : k * 128 + j * 8 + 8] for j in range(NC) for k in range(2)], axis=0
        ).astype(BF)

    ks_send[...] = nt(xT[other], lgN[...]).astype(BF)
    sib_k = Copies(
        open_copies, lambda d: remote(ks_send, ks_recv, send.at[2], recv.at[2], sib), [0],
        (ks_send, send.at[2]), (ks_recv, recv.at[2]),
    )
    sib_k.start_all()
    ksum[...] = nt(xT[core], lgN[...])
    sib_k.wait_recv()
    ksum[...] += ks_recv[...].astype(F32)

    def fk_copy(d):
        j = ahead(d)
        return remote(kpk.at[j], karr.at[d], send.at[13], recv.at[13], {"ctx": j * 2 + core})

    fk = Copies(open_copies, fk_copy, PLANE, (kpk.at[0 : NC - 1], send.at[13]), (karr.at[1:NC], recv.at[13]))

    for j in range(NC):
        kpk[j] = ksum[j * 32 : j * 32 + 32, :].astype(BF)
    fk.start_all()

    for t in range(T // 128):
        at = slice(t * 128, (t + 1) * 128)
        tgs[at, :] = (tn(lgH[:, at], keysT[...]) + tn(dispH[:, at], sif[...])).astype(BF)

    for copies in open_copies:
        if copies is not fk:
            copies.drain()
    fk.wait_recv()
    acc = add_all(ksum[pl.ds(pl.multiple_of(chip * 32, 32), 32), :], karr, NC)
    kz[...] = acc.astype(BF)

    def fz_copy(e):
        return remote(kz, kzarr.at[e], send.at[14], recv.at[14], {"dp": zahead(e)})

    fz = Copies(open_copies, fz_copy, LINE, (kzarr.at[0 : NZ - 1], send.at[14]), (kzarr.at[1:NZ], recv.at[14]))


    fz.start_all()

    fk.drain()
    fz.wait_recv()
    kout[...] = add_all(acc, kzarr, NZ)

    for copies in open_copies:
        copies.drain()


def store_kernel(tgs, kout, wigs, wogs, tg_hbm, kg_hbm, wig_hbm, wog_hbm, st):
    pairs = ((wigs, wig_hbm), (wogs, wog_hbm), (tgs, tg_hbm), (kout, kg_hbm))
    copies = [pltpu.make_async_copy(src, dst, st.at[i]) for i, (src, dst) in enumerate(pairs)]
    for copy in copies:
        copy.start()
    for copy in copies:
        copy.wait()


def per_device(tokens, slot_keys, w_in, w_out, out_grad):
    hbm = pl.BlockSpec(memory_space=pltpu.HBM)
    vmem = pltpu.VMEM
    half = D // 2
    held = pl.pallas_call(
        kernel,
        out_shape=(
            pltpu.VMEM((T, D), BF),
            pltpu.VMEM((32, S), F32),
            pltpu.VMEM((2, D, HL), BF),
            pltpu.VMEM((2, HL, D), BF),
        ),
        in_specs=[hbm] * 5,
        out_specs=(pl.BlockSpec(memory_space=vmem),) * 4,
        scratch_shapes=[
            vmem((T, D), BF), vmem((D, S), BF), vmem((2, D, HL), BF), vmem((2, HL, D), BF), vmem((T, D), BF),
            vmem((S, D), BF), vmem((S, T), F32), vmem((S, T), F32), vmem((S, T), BF), vmem((S, T), BF),
            vmem((2, D // 2, T), BF),
            vmem((128, D), BF), vmem((128, D), BF), vmem((128, D), F32),
            vmem((NC, 16, half), BF), vmem((NC, 16, half), BF),
            vmem((128, D + 128), BF), vmem((128, D + 128), BF), vmem((128, D), F32), vmem((S, 128), F32),
            vmem((NC, 16, half), BF), vmem((NC, 16, half), BF),
            vmem((2, 128), F32), vmem((NC, 2, 128), F32), vmem((128, 128), F32),
            vmem((2, HL, D), BF), vmem((2, D, HL), BF),
            vmem((16, half), F32), vmem((NZ, 16, half), BF), vmem((NZ, 16, half), BF),
            vmem((64, D), BF), vmem((64, D), BF), vmem((64, HL), F32),
            vmem((2, 64, HL), BF), vmem((2, 64, HL), BF), vmem((64, D), F32),
            vmem((NZ, 16, half), BF), vmem((NZ, 16, half), BF),
            vmem((NZ, 16, half), BF), vmem((NZ, 16, half), BF),
            vmem((2, NC, 16, half), BF), vmem((2, NC, 16, half + 128), BF), vmem((2, NC, 16, 128), BF),
            vmem((S, D), BF), vmem((S, D), BF),
            vmem((S, T), F32), vmem((S, T), BF), vmem((S, T), BF), vmem((S, T), BF),
            vmem((D // 2, S), BF), vmem((D // 2, S), BF), vmem((D // 2, S), F32),
            vmem((NC, 32, S), BF), vmem((NC, 32, S), BF), vmem((32, S), BF), vmem((NZ, 32, S), BF),
            pltpu.SemaphoreType.DMA((5,)), pltpu.SemaphoreType.DMA((18,)), pltpu.SemaphoreType.DMA((17,)),
            pltpu.SemaphoreType.DMA((NC,)), pltpu.SemaphoreType.DMA((NC,)), pltpu.SemaphoreType.DMA((NC,)),
        ],
        compiler_params=pltpu.CompilerParams(
            collective_id=0, has_side_effects=True, vmem_limit_bytes=36 * 2**20
        ),
        cost_estimate=pl.CostEstimate(flops=4 * 10**9, bytes_accessed=13 * 10**6, transcendentals=10**6),
    )(*(pltpu.with_memory_space_constraint(a, pltpu.HBM) for a in (tokens[0], slot_keys, w_in, w_out, out_grad[0])))
    tg, kg, wig, wog = pl.pallas_call(
        store_kernel,
        out_shape=(
            pltpu.HBM((T, D), BF),
            pltpu.HBM((32, S), F32),
            pltpu.HBM((2, D, HL), BF),
            pltpu.HBM((2, HL, D), BF),
        ),
        in_specs=[pl.BlockSpec(memory_space=vmem)] * 4,
        out_specs=(hbm,) * 4,
        scratch_shapes=[pltpu.SemaphoreType.DMA((4,))],
        compiler_params=pltpu.CompilerParams(vmem_limit_bytes=2**20),
    )(*held)
    return tg[None], kg, wig, wog


def solution(mesh):
    return jax.shard_map(
        per_device,
        mesh=mesh,
        in_specs=(
            P("dp", "ctx", None),
            P(),
            P("ctx", None, "dp"),
            P("ctx", "dp", None),
            P("dp", "ctx", None),
        ),
        out_specs=(
            P("dp", "ctx", None),
            P("ctx", None),
            P("ctx", None, "dp"),
            P("ctx", "dp", None),
        ),
        check_vma=False,
    )
```
